32 devices in a mesh: gx: 4 (over y, core), gy: 4 (over z), gz: 2 (over x).
Axes of the slice: x: 2, y: 2, z: 4, core: 2. Of those that a mesh axis runs over, the one named last changes fastest.
Arguments:
- positions: float32 [4, 4, 2, 3, 256], P('gx', 'gy', 'gz'), may hold values from 0.3 to 7.7, as said below
- velocities: float32 [4, 4, 2, 3, 256], P('gx', 'gy', 'gz'), may hold values from -6 to 6
- species: int32 [4, 4, 2, 256], P('gx', 'gy', 'gz'), may hold values from 0 to 3
- pair_table: int32 [4, 4, 2, 3, 1536], P('gx', 'gy', 'gz'), may hold values from 0 to 6911, as said below
- live_blocks: int32 [4, 4, 2], P('gx', 'gy', 'gz'), may hold values from 6 to 12, as said below
- owners: int32 [4, 4, 2, 2], P('gx', 'gy', 'gz'), may hold values from 0 to 1, as said below
- radial_weight: float32 [256, 8], replicated, may hold values from -2 to 2
- center_embed: float32 [256, 4], replicated, may hold values from -3 to 3
- neighbour_embed: float32 [256, 4], replicated, may hold values from -3 to 3
- vector_weight: float32 [32, 8], replicated, may hold values from -2 to 2
- env_weight: float32 [2, 32, 256], replicated, may hold values from -0.375 to 0.375
- vector_gate: float32 [32, 256], replicated, may hold values from -0.375 to 0.375
- latent_weight: float32 [2, 256, 288], replicated, may hold values from -0.375 to 0.375
- energy_weight: float32 [256], replicated, may hold values from -0.375 to 0.375
Outputs:
- migrated: float32 [4, 4, 2, 2, 9, 128], P('gx', 'gy', 'gz')
The draws below stay inside these ranges and needn't reach their ends.
Inputs may be any that keep to these rules, and one draw needn't show every extreme that they name: `positions`: atom k of a domain lies within 0.2 in each coordinate of the point (ix + 0.5, iy + 0.5, iz + 0.5) with k = (8 ix + iy) (4) + iz. `pair_table`: row 0 is a centre atom index below 256; row 1 a neighbour index as in the statement, never the centre itself; row 2 equals the species of that neighbour atom in its own domain. `live_blocks`: some device uses all 12 blocks. The owners of one device's blocks are distinct; in every gz group some device is the owner of one block of every device of the group.
All inputs are finite; a program needn't handle non-finite values.
Results may differ from the reference program's by a relative error of at most 0.0003.
Values sent between devices are 32-bit elements; how exact they have to be, the bound alone decides.
A program may use at most 64 MiB of HBM per device.

```python
import jax
import jax.numpy as jnp
from jax import lax

LATENT = 256
CHANNELS = 32
RADIAL = 8
SPECIES = 4
LAYERS = 2
BLOCKS = 2
PAIR_BLOCKS = 12
ATOMS_DEV = 256
XDOMAINS = 4
YDOMAINS = 4
ZDOMAINS = 2


def species_common(key):
    return jax.random.randint(jax.random.fold_in(key, 7), (XDOMAINS, YDOMAINS, ZDOMAINS, 128 * BLOCKS), 0, SPECIES)


def draw_species(key, part):
    return species_common(key)


def draw_positions(key, part):
    atoms_here = 128 * BLOCKS
    depth = atoms_here // 64
    labels = jnp.arange(atoms_here)
    lattice = jnp.stack([labels // (8 * depth), labels // depth % 8, labels % depth]).astype(jnp.float32) + 0.5
    shape = (XDOMAINS, YDOMAINS, ZDOMAINS, 3, atoms_here)
    jitter = jnp.clip(0.08 * jax.random.normal(jax.random.fold_in(key, 3), shape, jnp.float32), -0.2, 0.2)
    return lattice + jitter


def draw_pair_table(key, part):
    atoms_here = 128 * BLOCKS
    depth = atoms_here // 64
    pair_count = 128 * PAIR_BLOCKS
    shape = (XDOMAINS, YDOMAINS, ZDOMAINS, pair_count)
    centres = jax.random.randint(jax.random.fold_in(key, 21), shape, 0, atoms_here)
    steps = jax.random.randint(jax.random.fold_in(key, 22), (3,) + shape, -2, 3)
    still = (steps[0] == 0) & (steps[1] == 0) & (steps[2] == 0)
    steps = steps.at[0].set(jnp.where(still, 1, steps[0]))
    cell_x = centres // (8 * depth) + steps[0]
    cell_y = centres // depth % 8 + steps[1]
    cell_z = centres % depth + steps[2]
    hop_x = jnp.floor_divide(cell_x, 8)
    hop_y = jnp.floor_divide(cell_y, 8)
    hop_z = jnp.floor_divide(cell_z, depth)
    local_x = cell_x - hop_x * 8
    local_y = cell_y - hop_y * 8
    local_z = cell_z - hop_z * depth
    slot_index = (hop_x + 1) * 9 + (hop_y + 1) * 3 + (hop_z + 1)
    atom_index = (local_x * 8 + local_y) * depth + local_z
    neighbour = slot_index * atoms_here + atom_index
    grid_x = jnp.arange(XDOMAINS)[:, None, None, None]
    grid_y = jnp.arange(YDOMAINS)[None, :, None, None]
    grid_z = jnp.arange(ZDOMAINS)[None, None, :, None]
    kinds = species_common(key)
    other = kinds[(grid_x + hop_x) % XDOMAINS, (grid_y + hop_y) % YDOMAINS, (grid_z + hop_z) % ZDOMAINS, atom_index]
    return jnp.stack([centres, neighbour, other], axis=3).astype(jnp.int32)


def draw_live_blocks(key, part):
    shape = (XDOMAINS, YDOMAINS, ZDOMAINS)
    counts = jax.random.randint(jax.random.fold_in(key, 31), shape, PAIR_BLOCKS // 2, PAIR_BLOCKS + 1)
    chosen = jax.random.randint(jax.random.fold_in(key, 32), (), 0, XDOMAINS * YDOMAINS * ZDOMAINS)
    flat = counts.reshape(-1)
    flat = jnp.where(jnp.arange(flat.shape[0]) == chosen, PAIR_BLOCKS, flat)
    return flat.reshape(shape).astype(jnp.int32)


def draw_owners(key, part):
    shape = (XDOMAINS, YDOMAINS, ZDOMAINS)
    receiver = jax.random.randint(jax.random.fold_in(key, 41), (XDOMAINS, YDOMAINS, 1), 0, ZDOMAINS)
    receiver = jnp.broadcast_to(receiver, shape)
    scores = jax.random.randint(jax.random.fold_in(key, 42), shape + (ZDOMAINS,), 0, 1 << 20) * ZDOMAINS + jnp.arange(ZDOMAINS)
    scores = jnp.where(jnp.arange(ZDOMAINS) == receiver[..., None], -1, scores)
    order = jnp.argsort(scores, axis=-1, stable=True)
    turn = jax.random.randint(jax.random.fold_in(key, 43), shape + (1,), 0, BLOCKS)
    picks = (jnp.arange(BLOCKS) + turn) % BLOCKS
    return jnp.take_along_axis(order, picks, axis=-1).astype(jnp.int32)


def levels(key, dims, pieces, smallest, top_value):
    def one(axis_at, blocks):
        draws = jax.random.uniform(jax.random.fold_in(jax.random.fold_in(key, 6), axis_at), (blocks,), jnp.float32, smallest / len(pieces), top_value / len(pieces))
        return jnp.repeat(jnp.exp(draws), dims[axis_at] // blocks).reshape((-1,) + (1,) * (len(dims) - axis_at - 1))

    level = one(*pieces[0])
    for cut in pieces[1:]:
        level = level * one(*cut)
    return level


def bell_draw(key, extent, width, bound, shards=(), kind=jnp.bfloat16):
    entries = width * jax.random.normal(key, extent, jnp.float32)
    if shards:
        entries = entries * levels(key, extent, shards, -0.22, 0.18)
    return jnp.clip(entries, -bound, bound).astype(kind)


def setup_inputs(seed: int = 0) -> dict:
    seeds = jax.random.split(jax.random.key(seed), 15)
    return {
        "positions": draw_positions(jax.random.fold_in(seeds[14], 71), 0),
        "velocities": bell_draw(seeds[1], (XDOMAINS, YDOMAINS, ZDOMAINS, 3, ATOMS_DEV), 1.0, 6.0, ((0, 4), (1, 4), (2, 2)), jnp.float32),
        "species": draw_species(jax.random.fold_in(seeds[14], 71), 0),
        "pair_table": draw_pair_table(jax.random.fold_in(seeds[14], 71), 0),
        "live_blocks": draw_live_blocks(jax.random.fold_in(seeds[14], 71), 0),
        "owners": draw_owners(jax.random.fold_in(seeds[14], 71), 0),
        "radial_weight": bell_draw(seeds[6], (LATENT, RADIAL), RADIAL ** -0.5, 2.0, (), jnp.float32),
        "center_embed": bell_draw(seeds[7], (LATENT, SPECIES), SPECIES ** -0.5, 3.0, (), jnp.float32),
        "neighbour_embed": bell_draw(seeds[8], (LATENT, SPECIES), SPECIES ** -0.5, 3.0, (), jnp.float32),
        "vector_weight": bell_draw(seeds[9], (CHANNELS, RADIAL), RADIAL ** -0.5, 2.0, (), jnp.float32),
        "env_weight": bell_draw(seeds[10], (LAYERS, CHANNELS, LATENT), LATENT ** -0.5, 0.375, (), jnp.float32),
        "vector_gate": bell_draw(seeds[11], (CHANNELS, LATENT), LATENT ** -0.5, 0.375, (), jnp.float32),
        "latent_weight": bell_draw(seeds[12], (LAYERS, LATENT, LATENT + CHANNELS), (LATENT + CHANNELS) ** -0.5, 0.375, (), jnp.float32),
        "energy_weight": bell_draw(seeds[13], (LATENT,), LATENT ** -0.5, 0.375, (), jnp.float32),
    }


CUTOFF = 5.0
ENV_SCALE = 0.4
TIME_STEP = 0.2

def matmul(left, right):
    return jnp.dot(left, right, precision=lax.Precision.HIGHEST)

def pair_energy(extended, pair_rows, live_count, own_species, radial_weight, center_embed, neighbour_embed, vector_weight, env_weight, vector_gate, latent_weight, energy_weight):
    atoms_here = own_species.shape[0]
    pair_count = pair_rows.shape[1]
    depth = atoms_here // 64
    centres = pair_rows[0]
    neighbour = pair_rows[1]
    other_species = pair_rows[2]
    slot_index = neighbour // atoms_here
    atom_index = neighbour - slot_index * atoms_here
    offset_x = (slot_index // 9 - 1).astype(jnp.float32) * 8.0
    offset_y = (slot_index // 3 % 3 - 1).astype(jnp.float32) * 8.0
    offset_z = (slot_index % 3 - 1).astype(jnp.float32) * float(depth)
    shifts = jnp.stack([offset_x, offset_y, offset_z])
    far_end = extended[slot_index, :, atom_index].T
    near_end = extended[13, :, centres].T
    displace = far_end + shifts - near_end
    distance = jnp.sqrt(lax.optimization_barrier(jnp.sum(displace * displace, axis=0)))
    unit = displace / distance
    orders = jnp.arange(1, radial_weight.shape[1] + 1).astype(jnp.float32)
    basis = jnp.sqrt(2.0 / CUTOFF) * jnp.sin(orders[:, None] * jnp.pi * distance[None] / CUTOFF) / distance[None]
    ratio = distance / CUTOFF
    in_use = (jnp.arange(pair_count) < live_count * 128).astype(jnp.float32)
    envelope = (1.0 - ratio * ratio) ** 2 * in_use
    kinds = jnp.arange(center_embed.shape[1])[:, None]
    centre_hot = (kinds == own_species[centres][None]).astype(jnp.float32)
    other_hot = (kinds == other_species[None]).astype(jnp.float32)
    latent = envelope[None] * jax.nn.silu(matmul(radial_weight, basis) + matmul(center_embed, centre_hot) + matmul(neighbour_embed, other_hot))
    channels = vector_weight.shape[0]
    vectors = envelope[None, None] * matmul(vector_weight, basis)[None] * unit[:, None, :]
    member = (centres[:, None] == jnp.arange(atoms_here)[None]).astype(jnp.float32)
    n_layers = env_weight.shape[0]
    for layer in range(n_layers):
        env_pairs = matmul(env_weight[layer], latent)
        spread = (unit[:, None, :] * env_pairs[None]).reshape(3 * channels, pair_count)
        environment = ENV_SCALE * matmul(spread, member)
        at_pairs = lax.dot_general(environment, member, (((1,), (1,)), ((), ())), precision=lax.Precision.HIGHEST)
        at_pairs = at_pairs.reshape(3, channels, pair_count)
        scalars = lax.optimization_barrier(jnp.sum(vectors * at_pairs, axis=0))
        update = matmul(latent_weight[layer], jnp.concatenate([latent, scalars], axis=0))
        if layer + 1 < n_layers:
            vectors = vectors + at_pairs * matmul(vector_gate, latent)[None]
        latent = latent + envelope[None] * jax.nn.silu(update)
    return jnp.sum(matmul(energy_weight[None], latent))

def reference(positions, velocities, species, pair_table, live_blocks, owners, radial_weight, center_embed, neighbour_embed, vector_weight, env_weight, vector_gate, latent_weight, energy_weight):
    xcount, ycount, zcount, _, atoms_here = positions.shape
    depth = atoms_here // 64
    padded = jnp.pad(positions, ((1, 1), (1, 1), (1, 1), (0, 0), (0, 0)), mode='wrap')

    def one_domain(flat):
        grid_x = flat // (ycount * zcount)
        grid_y = flat // zcount % ycount
        grid_z = flat % zcount
        zero = grid_x * 0
        block = lax.dynamic_slice(padded, (grid_x, grid_y, grid_z, zero, zero), (3, 3, 3, 3, atoms_here))
        extended = block.reshape(27, 3, atoms_here)
        grad = jax.grad(pair_energy)(extended, pair_table[grid_x, grid_y, grid_z], live_blocks[grid_x, grid_y, grid_z], species[grid_x, grid_y, grid_z], radial_weight, center_embed, neighbour_embed, vector_weight, env_weight, vector_gate, latent_weight, energy_weight)
        return grad.reshape(3, 3, 3, 3, atoms_here)
    grads = lax.map(one_domain, jnp.arange(xcount * ycount * zcount, dtype=jnp.int32))
    grads = grads.reshape(xcount, ycount, zcount, 3, 3, 3, 3, atoms_here)
    forces = jnp.zeros((xcount, ycount, zcount, 3, atoms_here), jnp.float32)
    for step_x in range(3):
        for step_y in range(3):
            for step_z in range(3):
                forces = forces - jnp.roll(grads[:, :, :, step_x, step_y, step_z], (step_x - 1, step_y - 1, step_z - 1), axis=(0, 1, 2))
    inverse_mass = 1.0 / (1.0 + species.astype(jnp.float32))
    new_vel = velocities + TIME_STEP * forces * inverse_mass[:, :, :, None, :]
    new_pos = positions + TIME_STEP * new_vel
    state = jnp.concatenate([new_pos, new_vel, forces], axis=3)
    blocks_count = atoms_here // 128
    blocks = state.reshape(xcount, ycount, zcount, 9, blocks_count, 128).transpose(0, 1, 2, 4, 3, 5)
    hits = (owners[..., None] == jnp.arange(zcount)).astype(jnp.float32)
    moved = jnp.einsum('xysbd,xysbcq->xydscq', hits, blocks, precision=lax.Precision.HIGHEST)
    flags = lax.optimization_barrier(jnp.sum(hits, axis=3)).transpose(0, 1, 3, 2)
    source = jnp.arange(zcount)[None, None, None, :]
    target = jnp.arange(zcount)[None, None, :, None]
    rise = flags * (source - target).astype(jnp.float32) * float(depth)
    moved = moved.at[:, :, :, :, 2, :].add(rise[..., None])
    return moved
```

```python
import functools

import jax
import jax.numpy as jnp
from jax import lax
from jax.experimental import pallas as pl
from jax.experimental.pallas import tpu as pltpu
from jax.sharding import PartitionSpec as P

CUTOFF = 5.0
ENV_SCALE = 0.4
TIME_STEP = 0.2
CHUNK = 256
SLOTS = 27
F32 = jnp.float32
BF16 = jnp.bfloat16
MESH = pl.DeviceIdType.MESH


def split(x):
    high = x.astype(BF16)
    return high, (x - high.astype(F32)).astype(BF16)


def split3(x):
    high = x.astype(BF16)
    rest = x - high.astype(F32)
    mid = rest.astype(BF16)
    return high, mid, (rest - mid.astype(F32)).astype(BF16)


def dot(a, b):
    return jnp.dot(a, b, preferred_element_type=F32)


def dot_t(a, b):
    return lax.dot_general(a, b, (((1,), (1,)), ((), ())), preferred_element_type=F32)


def mul3(w_high, w_low, x):
    high, low = split(x)
    return dot(w_high, high) + dot(w_high, low) + dot(w_low, high)


def wide(x, lanes):
    if x.shape[1] == lanes:
        return x
    return jnp.concatenate([x, jnp.zeros((x.shape[0], lanes - x.shape[1]), x.dtype)], axis=1)


def tall(x, rows):
    if x.shape[0] == rows:
        return x
    return jnp.concatenate([x, jnp.zeros((rows - x.shape[0], x.shape[1]), x.dtype)], axis=0)


def stack3(x):
    high, low = split(x)
    rows = 3 * x.shape[0]
    pad = -rows % 128
    parts = [high.astype(F32), low.astype(F32), high.astype(F32)]
    if pad:
        parts.append(jnp.zeros((pad, x.shape[1]), F32))
    return jnp.concatenate(parts, axis=0).astype(BF16)


def pack3(transposed):
    high, low = split(transposed)
    high, low = high.astype(F32), low.astype(F32)
    rows = 3 * transposed.shape[0]
    stacked = tall(jnp.concatenate([high, high, low], axis=0), rows + (-rows % 128))
    return stacked.T.astype(BF16)


def silu_pair(x):
    gate = 0.5 + 0.5 * jnp.tanh(0.5 * x)
    value = x * gate
    return value, gate + value * (1.0 - gate)


def rows3(x):
    n = x.shape[0] // 3
    return x[:n], x[n : 2 * n], x[2 * n :]


def prepare(weights, scratch):
    radial, centre_e, neigh_e, vector, env_w, gate_w, latent_w, energy = weights
    (w_first, wa_h, wa_l, wb_h, wb_l, s0, s1, t0_h, t0_l, t1_h, t1_l, gate_t, e0_t, e1_t, back_h, back_l, ew) = scratch
    width = radial.shape[0]
    channels = vector.shape[0]
    radial_t = wide(radial[...], 128).T[:8]
    centre_t = wide(centre_e[...], 128).T[:8]
    neigh_t = wide(neigh_e[...], 128).T[:8]
    vector_t = wide(tall(vector[...], 128), 128).T[:8, :channels]
    zeros = jnp.zeros((8, 128), F32)
    vector_tp = wide(vector_t, 128)
    first_t = jnp.concatenate(
        [
            jnp.concatenate([radial_t, vector_tp], axis=1),
            jnp.concatenate([centre_t, zeros], axis=1),
            jnp.concatenate([neigh_t, zeros], axis=1),
        ],
        axis=0,
    )
    w_first[...] = pack3(first_t)
    layer0 = wide(latent_w[0], 384).T
    layer1 = wide(latent_w[1], 384).T
    high, low = split(jnp.concatenate([latent_w[0][:, :width], gate_w[...], env_w[0]], axis=0))
    wa_h[...], wa_l[...] = high, low
    high, low = split(jnp.concatenate([latent_w[1][:, :width], env_w[1]], axis=0))
    wb_h[...], wb_l[...] = high, low
    s0[...] = pack3(layer0[width : width + channels])
    s1[...] = pack3(layer1[width : width + channels])
    t0_h[...], t0_l[...] = split(layer0[: width + channels])
    t1_h[...], t1_l[...] = split(layer1[: width + channels])
    gate_t[...] = pack3(gate_w[...])
    e0_t[...] = pack3(env_w[0])
    e1_t[...] = pack3(env_w[1])
    back = tall(jnp.concatenate([radial_t, vector_tp], axis=1), 16)
    back_h[...], back_l[...] = split(back)
    ew[...] = jnp.broadcast_to(tall(energy[...], 8).T[:, :1], (width, 128))


def hot_matrices(pair, mem_t, nbr_t, atoms):
    count = pair.shape[1]
    labels = lax.broadcasted_iota(jnp.int32, (atoms, CHUNK), 0)

    def chunk(i, carry):
        here = pl.ds(pl.multiple_of(i * CHUNK, CHUNK), CHUNK)
        centre = pair[0:1, here]
        atom = pair[1:2, here] & (atoms - 1)
        mem_t[:, here] = (labels == centre).astype(F32).astype(BF16)
        nbr_t[:, here] = (labels == atom).astype(F32).astype(BF16)
        return carry

    lax.fori_loop(0, count // CHUNK, chunk, 0)


def sum3(values, by):
    a, b, c = rows3(values)
    return a * by[0:1] + b * by[1:2] + c * by[2:3]


def times3(by, value):
    return jnp.concatenate([value * by[0:1], value * by[1:2], value * by[2:3]], axis=0)


def tile3(value):
    return jnp.concatenate([value, value, value], axis=0)


def fold3(values):
    a, b, c = rows3(values)
    return a + b + c


def sums3(values):
    a, b, c = rows3(values)
    return jnp.concatenate(
        [jnp.sum(a, axis=0, keepdims=True), jnp.sum(b, axis=0, keepdims=True), jnp.sum(c, axis=0, keepdims=True)],
        axis=0,
    )


def gradient(table, near_table, pair, live, weights, hots, store):
    (w_first, wa_h, wa_l, wb_h, wb_l, s0, s1, t0_h, t0_l, t1_h, t1_l, gate_t, e0_t, e1_t, back_h, back_l, ew) = weights
    mem_t, nbr_t = hots
    (geo, trig, silu0, dsilu0, upper, lower, silu1, dsilu1, small, at0s, v1s, dv1s, dlat, acc, spread_acc) = store
    atoms, count = mem_t.shape
    depth = float(atoms // 64)
    width = silu0.shape[0]
    ch = v1s.shape[0] // 3
    steps = count // CHUNK
    slot_rows = lax.broadcasted_iota(jnp.int32, (32, CHUNK), 0)
    lanes = lax.broadcasted_iota(jnp.int32, (1, CHUNK), 1)
    orders = (lax.broadcasted_iota(jnp.int32, (8, CHUNK), 0) + 1).astype(F32)
    kinds = lax.broadcasted_iota(jnp.int32, (8, CHUNK), 0)
    vw, vb, g0, ep0, ep1, dvw = (slice(k * ch, (k + 1) * ch) for k in range(6))

    def at(i):
        return pl.ds(pl.multiple_of(i * CHUNK, CHUNK), CHUNK)

    def loop(body):
        acc[...] = jnp.zeros_like(acc)
        lax.fori_loop(0, steps, lambda i, c: (body(at(i), i), c)[1], 0)
        total = acc[...]
        n = total.shape[0] // 2
        high, low = split(ENV_SCALE * (total[:n] + total[n:]))
        return jnp.concatenate([high, low], axis=0)

    def gather(two, here):
        both = dot(two, mem_t[:, here])
        n = both.shape[0] // 2
        return both[:n] + both[n:]

    def scatter(values, here):
        high, low = split(values)
        acc[...] += dot_t(jnp.concatenate([high, low], axis=0), mem_t[:, here])

    def energy_rows():
        value = ew[...]
        return jnp.concatenate([value] * (CHUNK // 128), axis=1)

    def phase_a(here, i):
        slot = pair[1:2, here] // atoms
        far = dot(table, nbr_t[:, here])
        far = far[:96] + far[96:192] + far[192:]
        hot = slot_rows == slot
        picks = [
            jnp.sum(jnp.where(hot, far[32 * m : 32 * m + 32], 0.0), axis=0, keepdims=True) for m in range(3)
        ]
        near = dot(near_table, mem_t[:, here])
        centre_hot = near[24:32]
        near = near[0:8] + near[8:16] + near[16:24]
        shift_x = (slot // 9 - 1).astype(F32) * 8.0
        shift_y = (slot // 3 % 3 - 1).astype(F32) * 8.0
        shift_z = (slot % 3 - 1).astype(F32) * depth
        dx = picks[0] + shift_x - near[0:1]
        dy = picks[1] + shift_y - near[1:2]
        dz = picks[2] + shift_z - near[2:3]
        distance = jnp.sqrt(dx * dx + dy * dy + dz * dz)
        inverse = 1.0 / distance
        unit = jnp.concatenate([dx, dy, dz], axis=0) * inverse
        ratio = distance / CUTOFF
        use = (i * CHUNK + lanes < live * 128).astype(F32)
        bump = 1.0 - ratio * ratio
        envelope = bump * bump * use
        slope = bump * use * (-4.0 / CUTOFF) * ratio
        angle = orders * jnp.pi * distance / CUTOFF
        norm = (2.0 / CUTOFF) ** 0.5 * inverse
        basis = norm * jnp.sin(angle)
        trig[:, here] = norm * (orders * (jnp.pi / CUTOFF)) * jnp.cos(angle) - basis * inverse
        geo[0:3, here] = unit
        geo[3:4, here] = envelope
        geo[4:5, here] = inverse
        geo[5:6, here] = slope
        other_hot = (kinds == pair[2:3, here]).astype(F32)
        first = dot(w_first[...], stack3(jnp.concatenate([basis, centre_hot, other_hot], axis=0)))
        value, deriv = silu_pair(first[:width])
        silu0[:, here] = value
        dsilu0[:, here] = deriv
        plain = first[width : width + ch]
        small[vb, here] = plain
        small[vw, here] = envelope * plain
        after = mul3(wa_h[...], wa_l[...], envelope * value)
        upper[:, here] = after[:width]
        small[g0, here] = after[width : width + ch]
        small[ep0, here] = after[width + ch :]
        scatter(times3(unit, after[width + ch :]), here)

    env0 = loop(phase_a)

    def phase_b(here, i):
        unit, envelope = geo[0:3, here], geo[3:4, here]
        at_pairs = gather(env0, here)
        at0s[:, here] = at_pairs
        vw_here = small[vw, here]
        scalars = vw_here * sum3(at_pairs, unit)
        update = upper[:, here] + dot(s0[...], stack3(scalars))
        value, deriv = silu_pair(update)
        silu1[:, here] = value
        dsilu1[:, here] = deriv
        v1s[:, here] = times3(unit, vw_here) + at_pairs * tile3(small[g0, here])
        after = mul3(wb_h[...], wb_l[...], envelope * (silu0[:, here] + value))
        lower[:, here] = after[:width]
        small[ep1, here] = after[width:]
        scatter(times3(unit, after[width:]), here)

    env1 = loop(phase_b)

    def phase_c(here, i):
        envelope = geo[3:4, here]
        at_pairs = gather(env1, here)
        vectors = v1s[:, here]
        update = lower[:, here] + dot(s1[...], stack3(fold3(vectors * at_pairs)))
        value, deriv = silu_pair(update)
        weight = energy_rows()
        geo[6:7, here] = jnp.sum(weight * value, axis=0, keepdims=True)
        back = mul3(t1_h[...], t1_l[...], weight * deriv * envelope)
        dlat[:, here] = weight + back[:width]
        d_scalar = tile3(back[width:])
        dv1s[:, here] = d_scalar * at_pairs
        scatter(d_scalar * vectors, here)

    denv1 = loop(phase_c)

    def phase_d(here, i):
        unit, envelope = geo[0:3, here], geo[3:4, here]
        d_spread = gather(denv1, here)
        d_unit = sums3(d_spread * tile3(small[ep1, here]))
        at_pairs = at0s[:, here]
        dv1 = dv1s[:, here]
        d_latent = dlat[:, here] + dot(e1_t[...], stack3(sum3(d_spread, unit)))
        d_gate = fold3(dv1 * at_pairs)
        back = mul3(t0_h[...], t0_l[...], d_latent * envelope * dsilu1[:, here])
        geo[6:7, here] = geo[6:7, here] + jnp.sum(d_latent * silu1[:, here], axis=0, keepdims=True)
        dlat[:, here] = d_latent + back[:width] + dot(gate_t[...], stack3(d_gate))
        d_scalar = back[width:]
        vw_here = small[vw, here]
        d_vectors = dv1 + tile3(d_scalar) * at_pairs
        small[dvw, here] = sum3(d_vectors, unit)
        geo[8:11, here] = d_unit + sums3(d_vectors * tile3(vw_here))
        scatter(dv1 * tile3(small[g0, here]) + times3(unit, d_scalar * vw_here), here)

    denv0 = loop(phase_d)
    spread_acc[...] = jnp.zeros_like(spread_acc)

    def phase_e(here, i):
        unit, envelope = geo[0:3, here], geo[3:4, here]
        d_spread = gather(denv0, here)
        d_unit = geo[8:11, here] + sums3(d_spread * tile3(small[ep0, here]))
        d_latent = dlat[:, here] + dot(e0_t[...], stack3(sum3(d_spread, unit)))
        d_vw = small[dvw, here]
        d_envelope = (
            geo[6:7, here]
            + jnp.sum(d_latent * silu0[:, here], axis=0, keepdims=True)
            + jnp.sum(d_vw * small[vb, here], axis=0, keepdims=True)
        )
        d_first = jnp.concatenate(
            [d_latent * envelope * dsilu0[:, here], tall(envelope * d_vw, 128)], axis=0
        )
        d_basis = mul3(back_h[...], back_l[...], d_first)[:8]
        d_distance = jnp.sum(d_basis * trig[:, here], axis=0, keepdims=True) + d_envelope * geo[5:6, here]
        along = jnp.sum(unit * d_unit, axis=0, keepdims=True)
        d_move = unit * d_distance + (d_unit - unit * along) * geo[4:5, here]
        hot = slot_rows == pair[1:2, here] // atoms
        high, low = split(
            jnp.concatenate([jnp.where(hot, d_move[m : m + 1], 0.0) for m in range(3)], axis=0)
        )
        spread_acc[0:192] += dot_t(jnp.concatenate([high, low], axis=0), nbr_t[:, here])
        high, low = split(tall(d_move, 16))
        spread_acc[192:224] += dot_t(jnp.concatenate([high, low], axis=0), mem_t[:, here])

    lax.fori_loop(0, steps, lambda i, c: (phase_e(at(i), i), c)[1], 0)
    by_slot = spread_acc[0:96] + spread_acc[96:192]
    by_centre = spread_acc[192:208] + spread_acc[208:224]
    return by_slot, by_centre


def weight_scratch(width, ch):
    def b(*shape):
        return pltpu.VMEM(shape, BF16)

    return [
        b(width + 128, 128),
        b(width + 2 * ch, width),
        b(width + 2 * ch, width),
        b(width + ch, width),
        b(width + ch, width),
        b(width, 128),
        b(width, 128),
        b(width + ch, width),
        b(width + ch, width),
        b(width + ch, width),
        b(width + ch, width),
        b(width, 128),
        b(width, 128),
        b(width, 128),
        b(16, width + 128),
        b(16, width + 128),
        pltpu.VMEM((width, 128), F32),
    ]


def store_scratch(width, ch, count, atoms):
    def f(*shape):
        return pltpu.VMEM(shape, F32)

    return [
        f(16, count),
        f(8, count),
        f(width, count),
        f(width, count),
        f(width, count),
        f(width, count),
        f(width, count),
        f(width, count),
        f(6 * ch, count),
        f(3 * ch, count),
        f(3 * ch, count),
        f(3 * ch, count),
        f(width, count),
        f(6 * ch, atoms),
        f(224, atoms),
    ]


def wrapped(step, size):
    return step % size


def kernel(
    sizes,
    live_ref,
    owner_ref,
    pos,
    vel,
    kind,
    pair,
    radial,
    centre_e,
    neigh_e,
    vector,
    env_w,
    gate_w,
    latent_w,
    energy,
    out,
    *scratch,
):
    xs, ys, zs = sizes
    weights = (radial, centre_e, neigh_e, vector, env_w, gate_w, latent_w, energy)
    w_scratch, store = scratch[:17], scratch[17:32]
    (mem_t, nbr_t, own, halo, force_out, force_in, move_out, move_in,
     pos_send, pos_recv, force_send, force_recv, move_send, move_recv) = scratch[32:]
    atoms = pos.shape[1]
    me = (lax.axis_index("gx"), lax.axis_index("gy"), lax.axis_index("gz"))

    def device(step):
        return tuple(lax.rem(m + s % n, n) for m, s, n in zip(me, step, sizes))

    slots = [(x, y, z) for x in (-1, 0, 1) for y in (-1, 0, 1) for z in (-1, 0, 1)]
    first = {}
    for k, s in enumerate(slots):
        first.setdefault((s[0] % xs, s[1] % ys, s[2] % zs), k)
    leader = [first[(s[0] % xs, s[1] % ys, s[2] % zs)] for s in slots]
    home = first[(0, 0, 0)]
    leaders = [k for k in first.values() if k != home]
    partners = {(s[0] % xs, s[1] % ys, s[2] % zs) for s in (slots[k] for k in leaders)}
    partners |= {((-x) % xs, (-y) % ys, (-z) % zs) for x, y, z in partners}
    partners |= {(0, 0, z) for z in range(1, zs)}
    partners = sorted(partners)

    barrier = pltpu.get_barrier_semaphore()
    for step in partners:
        pl.semaphore_signal(barrier, inc=1, device_id=device(step), device_id_type=MESH)
    here = pos[...]
    for m in range(3):
        own[0, :, m * atoms : (m + 1) * atoms] = here[m : m + 1]
    pl.semaphore_wait(barrier, len(partners))

    def push(k, source, target, send, recv, step):
        return pltpu.make_async_remote_copy(
            src_ref=source, dst_ref=target, send_sem=send.at[k], recv_sem=recv.at[k],
            device_id=device(step), device_id_type=MESH,
        )

    pos_copies = [
        push(k, own.at[0], halo.at[k], pos_send, pos_recv, tuple(-v for v in slots[k])) for k in leaders
    ]
    for copy in pos_copies:
        copy.start()

    prepare(weights, w_scratch)
    hot_matrices(pair, mem_t, nbr_t, atoms)
    species_hot = (
        lax.broadcasted_iota(jnp.int32, (8, atoms), 0) == kind[...]
    ).astype(F32)
    high, mid, low = (v.astype(F32) for v in split3(tall(here, 8)))
    near_table = jnp.concatenate([high, mid, low, species_hot], axis=0).astype(BF16)

    for copy in pos_copies:
        copy.wait()
    rows = []
    for m in range(3):
        cut = slice(m * atoms, (m + 1) * atoms)
        for k in range(SLOTS):
            rows.append(own[0, :, cut] if leader[k] == home else halo[leader[k], :, cut])
        rows.append(jnp.zeros((32 - SLOTS, atoms), F32))
    table = jnp.concatenate(split3(jnp.concatenate(rows, axis=0)), axis=0)

    by_slot, by_centre = gradient(
        table, near_table, pair, live_ref[0], w_scratch, (mem_t, nbr_t), store
    )

    members = {k: [j for j in range(SLOTS) if leader[j] == k] for k in leaders + [home]}

    def piece(k):
        parts = []
        for m in range(3):
            row = by_slot[32 * m + k : 32 * m + k + 1]
            for j in members[k][1:]:
                row = row + by_slot[32 * m + j : 32 * m + j + 1]
            parts.append(row)
        return parts

    force_copies = []
    for k in leaders:
        for m, row in enumerate(piece(k)):
            force_out[k, :, m * atoms : (m + 1) * atoms] = row
        copy = push(k, force_out.at[k], force_in.at[k], force_send, force_recv, slots[k])
        copy.start()
        force_copies.append(copy)
    total = jnp.concatenate(piece(home), axis=0) - by_centre[0:3]
    inverse_mass = 1.0 / (1.0 + kind[...].astype(F32))
    velocity = vel[...]
    for copy in force_copies:
        copy.wait()
    arrived = force_in[leaders[0]]
    for k in leaders[1:]:
        arrived = arrived + force_in[k]
    total = total + jnp.concatenate(
        [arrived[:, m * atoms : (m + 1) * atoms] for m in range(3)], axis=0
    )
    forces = -total
    new_vel = velocity + TIME_STEP * forces * inverse_mass
    new_pos = here + TIME_STEP * new_vel
    state = jnp.concatenate([new_pos, new_vel, forces], axis=0)
    blocks = atoms // 128
    depth = float(atoms // 64)
    is_z = (lax.broadcasted_iota(jnp.int32, (9, 128), 0) == 2).astype(F32)

    def block_for(target):
        result = jnp.zeros((9, 128), F32)
        lift = (me[2] - target).astype(F32) * depth
        for b in range(blocks):
            mine = jnp.full((9, 128), owner_ref[b], jnp.int32) == target
            result = result + jnp.where(mine, state[:, 128 * b : 128 * b + 128] + is_z * lift, 0.0)
        return result

    move_copies = []
    for z in range(1, zs):
        target = lax.rem(me[2] + z, zs)
        move_out[z] = block_for(target)
        copy = push(z, move_out.at[z], move_in.at[z], move_send, move_recv, (0, 0, z))
        copy.start()
        move_copies.append(copy)
    out[me[2]] = block_for(me[2])
    for copy in move_copies:
        copy.wait()
    for z in range(1, zs):
        source = lax.rem(me[2] + zs - z, zs)
        out[source] = move_in[z]


def per_device(
    sizes,
    positions,
    velocities,
    species,
    pair_table,
    live_blocks,
    owners,
    radial_weight,
    center_embed,
    neighbour_embed,
    vector_weight,
    env_weight,
    vector_gate,
    latent_weight,
    energy_weight,
):
    atoms = positions.shape[4]
    count = pair_table.shape[4]
    width = latent_weight.shape[1]
    ch = vector_weight.shape[0]
    zs = sizes[2]
    smem = pl.BlockSpec(memory_space=pltpu.SMEM)
    vmem = pl.BlockSpec(memory_space=pltpu.VMEM)
    dma = pltpu.SemaphoreType.DMA
    result = pl.pallas_call(
        functools.partial(kernel, sizes),
        out_shape=jax.ShapeDtypeStruct((zs, 9, 128), F32),
        in_specs=[smem, smem] + [vmem] * 12,
        out_specs=vmem,
        scratch_shapes=weight_scratch(width, ch)
        + store_scratch(width, ch, count, atoms)
        + [
            pltpu.VMEM((atoms, count), BF16),
            pltpu.VMEM((atoms, count), BF16),
            pltpu.VMEM((1, 1, 3 * atoms), F32),
            pltpu.VMEM((SLOTS, 1, 3 * atoms), F32),
            pltpu.VMEM((SLOTS, 1, 3 * atoms), F32),
            pltpu.VMEM((SLOTS, 1, 3 * atoms), F32),
            pltpu.VMEM((zs, 9, 128), F32),
            pltpu.VMEM((zs, 9, 128), F32),
            dma((SLOTS,)),
            dma((SLOTS,)),
            dma((SLOTS,)),
            dma((SLOTS,)),
            dma((zs,)),
            dma((zs,)),
        ],
        compiler_params=pltpu.CompilerParams(
            collective_id=0, has_side_effects=True, vmem_limit_bytes=48 << 20
        ),
    )(
        live_blocks.reshape(1),
        owners.reshape(-1),
        positions.reshape(3, atoms),
        velocities.reshape(3, atoms),
        species.reshape(1, atoms),
        pair_table.reshape(3, count),
        radial_weight,
        center_embed,
        neighbour_embed,
        vector_weight,
        env_weight,
        vector_gate,
        latent_weight,
        energy_weight.reshape(1, width),
    )
    return result[None, None, None]


def solution(mesh):
    sizes = (mesh.shape["gx"], mesh.shape["gy"], mesh.shape["gz"])
    spread = ("gx", "gy", "gz")
    in_specs = (
        P(*spread, None, None),
        P(*spread, None, None),
        P(*spread, None),
        P(*spread, None, None),
        P(*spread),
        P(*spread, None),
    ) + (P(),) * 8
    return jax.shard_map(
        functools.partial(per_device, sizes),
        mesh=mesh,
        in_specs=in_specs,
        out_specs=P(*spread, None, None, None),
        check_vma=False,
    )
```

```python
import functools

import jax
import jax.numpy as jnp
from jax import lax
from jax.experimental import pallas as pl
from jax.experimental.pallas import tpu as pltpu
from jax.sharding import PartitionSpec as P

CUTOFF = 5.0
ENV_SCALE = 0.4
TIME_STEP = 0.2
CHUNK = 512
SLOTS = 27
F32 = jnp.float32
BF16 = jnp.bfloat16
MESH = pl.DeviceIdType.MESH


def split(x):
    high = x.astype(BF16)
    return high, (x - high.astype(F32)).astype(BF16)


def split3(x):
    high = x.astype(BF16)
    rest = x - high.astype(F32)
    mid = rest.astype(BF16)
    return high, mid, (rest - mid.astype(F32)).astype(BF16)


def dot(a, b):
    return jnp.dot(a, b, preferred_element_type=F32)


def dot_t(a, b):
    return lax.dot_general(a, b, (((1,), (1,)), ((), ())), preferred_element_type=F32)


def mul3(w_high, w_low, x):
    high, low = split(x)
    return dot(w_high, high) + dot(w_high, low) + dot(w_low, high)


def wide(x, lanes):
    if x.shape[1] == lanes:
        return x
    return jnp.concatenate([x, jnp.zeros((x.shape[0], lanes - x.shape[1]), x.dtype)], axis=1)


def tall(x, rows):
    if x.shape[0] == rows:
        return x
    return jnp.concatenate([x, jnp.zeros((rows - x.shape[0], x.shape[1]), x.dtype)], axis=0)


def stack3(x):
    high, low = split(x)
    rows = 3 * x.shape[0]
    pad = -rows % 128
    parts = [high.astype(F32), low.astype(F32), high.astype(F32)]
    if pad:
        parts.append(jnp.zeros((pad, x.shape[1]), F32))
    return jnp.concatenate(parts, axis=0).astype(BF16)


def pack3(transposed):
    high, low = split(transposed)
    high, low = high.astype(F32), low.astype(F32)
    rows = 3 * transposed.shape[0]
    stacked = tall(jnp.concatenate([high, high, low], axis=0), rows + (-rows % 128))
    return stacked.T.astype(BF16)


def silu_pair(x):
    gate = 0.5 + 0.5 * jnp.tanh(0.5 * x)
    value = x * gate
    return value, gate + value * (1.0 - gate)


def rows3(x):
    n = x.shape[0] // 3
    return x[:n], x[n : 2 * n], x[2 * n :]


def prepare(weights, scratch):
    radial, centre_e, neigh_e, vector, env_w, gate_w, latent_w, energy = weights
    (w_first, wa_h, wa_l, wb_h, wb_l, s0, s1, t0_h, t0_l, t1_h, t1_l, gate_t, e0_t, e1_t, back_h, back_l, ew) = scratch
    width = radial.shape[1]
    channels = vector.shape[1]
    radial_t = radial[...]
    centre_t = tall(centre_e[...], 8)
    neigh_t = tall(neigh_e[...], 8)
    vector_t = vector[...]
    zeros = jnp.zeros((8, 128), F32)
    vector_tp = wide(vector_t, 128)
    first_t = jnp.concatenate(
        [
            jnp.concatenate([radial_t, vector_tp], axis=1),
            jnp.concatenate([centre_t, zeros], axis=1),
            jnp.concatenate([neigh_t, zeros], axis=1),
        ],
        axis=0,
    )
    w_first[...] = pack3(first_t)
    layer0, layer1 = latent_w[0], latent_w[1]
    high, low = split(jnp.concatenate([layer0[:width].T, gate_w[...], env_w[0]], axis=0))
    wa_h[...], wa_l[...] = high, low
    high, low = split(jnp.concatenate([layer1[:width].T, env_w[1]], axis=0))
    wb_h[...], wb_l[...] = high, low
    s0[...] = pack3(layer0[width : width + channels])
    s1[...] = pack3(layer1[width : width + channels])
    t0_h[...], t0_l[...] = split(layer0)
    t1_h[...], t1_l[...] = split(layer1)
    gate_t[...] = pack3(gate_w[...])
    e0_t[...] = pack3(env_w[0])
    e1_t[...] = pack3(env_w[1])
    back = tall(jnp.concatenate([radial_t, vector_tp], axis=1), 16)
    back_h[...], back_l[...] = split(back)
    ew[...] = jnp.broadcast_to(tall(energy[...], 8).T[:, :1], (width, 128))


def hot_matrices(pair, mem_t, nbr_t, atoms):
    count = pair.shape[2]
    labels = lax.broadcasted_iota(jnp.int32, (atoms, CHUNK), 0)

    def chunk(i, carry):
        here = pl.ds(pl.multiple_of(i * CHUNK, CHUNK), CHUNK)
        centre = pair[0, :, here]
        atom = pair[1, :, here] & (atoms - 1)
        mem_t[:, here] = (labels == centre).astype(F32).astype(BF16)
        nbr_t[:, here] = (labels == atom).astype(F32).astype(BF16)
        return carry

    lax.fori_loop(0, count // CHUNK, chunk, 0)


def sum3(values, by):
    a, b, c = rows3(values)
    return a * by[0:1] + b * by[1:2] + c * by[2:3]


def times3(by, value):
    return jnp.concatenate([value * by[0:1], value * by[1:2], value * by[2:3]], axis=0)


def tile3(value):
    return jnp.concatenate([value, value, value], axis=0)


def fold3(values):
    a, b, c = rows3(values)
    return a + b + c


def sums3(values):
    a, b, c = rows3(values)
    return jnp.concatenate(
        [jnp.sum(a, axis=0, keepdims=True), jnp.sum(b, axis=0, keepdims=True), jnp.sum(c, axis=0, keepdims=True)],
        axis=0,
    )


def gradient(table, near, pair, live, weights, hots, store):
    (w_first, wa_h, wa_l, wb_h, wb_l, s0, s1, t0_h, t0_l, t1_h, t1_l, gate_t, e0_t, e1_t, back_h, back_l, ew) = weights
    mem_t, nbr_t = hots
    (geo, trig, silu0, dsilu0, upper, lower, silu1, dsilu1, small, at0s, v1s, dv1s, dlat, acc, firsts, d_bases) = store
    atoms, count = mem_t.shape
    depth = float(atoms // 64)
    width = silu0.shape[0]
    ch = v1s.shape[0] // 3
    steps = count // CHUNK
    vw, vb, g0, ep0, ep1, dvw = (slice(k * ch, (k + 1) * ch) for k in range(6))

    def at(i):
        return pl.ds(pl.multiple_of(i * CHUNK, CHUNK), CHUNK)

    def loop(body):
        acc[...] = jnp.zeros_like(acc)
        lax.fori_loop(0, steps, lambda i, c: (body(at(i), i), c)[1], 0)
        total = acc[...]
        n = total.shape[0] // 2
        high, low = split(ENV_SCALE * (total[:n] + total[n:]))
        return jnp.concatenate([high, low], axis=0)

    def gather(two, here):
        both = dot(two, mem_t[:, here])
        n = both.shape[0] // 2
        return both[:n] + both[n:]

    def scatter(values, here):
        high, low = split(values)
        acc[...] += dot_t(jnp.concatenate([high, low], axis=0), mem_t[:, here])

    def energy_rows():
        value = ew[...]
        return jnp.concatenate([value] * (CHUNK // 128), axis=1)

    slot = pair[1] // atoms
    hot = lax.broadcasted_iota(jnp.int32, (32, count), 0) == slot
    far = dot(table, nbr_t[...])
    far = far[:96] + far[96:192] + far[192:]
    picks = [jnp.sum(jnp.where(hot, far[32 * m : 32 * m + 32], 0.0), axis=0, keepdims=True) for m in range(3)]
    dx = picks[0] + (slot // 9 - 1).astype(F32) * 8.0 - near[0:1]
    dy = picks[1] + (slot // 3 % 3 - 1).astype(F32) * 8.0 - near[1:2]
    dz = picks[2] + (slot % 3 - 1).astype(F32) * depth - near[2:3]
    distance = jnp.sqrt(dx * dx + dy * dy + dz * dz)
    inverse = 1.0 / distance
    ratio = distance / CUTOFF
    lanes = lax.broadcasted_iota(jnp.int32, (1, count), 1)
    use = (lanes < live * 128).astype(F32)
    bump = 1.0 - ratio * ratio
    geo[0:3] = jnp.concatenate([dx, dy, dz], axis=0) * inverse
    geo[3:4] = bump * bump * use
    geo[4:5] = inverse
    geo[5:6] = bump * use * (-4.0 / CUTOFF) * ratio
    orders = (lax.broadcasted_iota(jnp.int32, (8, count), 0) + 1).astype(F32)
    angle = orders * jnp.pi * distance / CUTOFF
    norm = (2.0 / CUTOFF) ** 0.5 * inverse
    basis = norm * jnp.sin(angle)
    trig[...] = norm * (orders * (jnp.pi / CUTOFF)) * jnp.cos(angle) - basis * inverse
    other_hot = (lax.broadcasted_iota(jnp.int32, (8, count), 0) == pair[2]).astype(F32)
    firsts[...] = stack3(jnp.concatenate([basis, near[8:16], other_hot], axis=0))

    def phase_a(here, i):
        unit, envelope = geo[0:3, here], geo[3:4, here]
        first = dot(w_first[...], firsts[:, here])
        value, deriv = silu_pair(first[:width])
        silu0[:, here] = value
        dsilu0[:, here] = deriv
        plain = first[width : width + ch]
        small[vb, here] = plain
        small[vw, here] = envelope * plain
        after = mul3(wa_h[...], wa_l[...], envelope * value)
        upper[:, here] = after[:width]
        small[g0, here] = after[width : width + ch]
        small[ep0, here] = after[width + ch :]
        scatter(times3(unit, after[width + ch :]), here)

    env0 = loop(phase_a)

    def phase_b(here, i):
        unit, envelope = geo[0:3, here], geo[3:4, here]
        at_pairs = gather(env0, here)
        at0s[:, here] = at_pairs
        vw_here = small[vw, here]
        scalars = vw_here * sum3(at_pairs, unit)
        update = upper[:, here] + dot(s0[...], stack3(scalars))
        value, deriv = silu_pair(update)
        silu1[:, here] = value
        dsilu1[:, here] = deriv
        v1s[:, here] = times3(unit, vw_here) + at_pairs * tile3(small[g0, here])
        after = mul3(wb_h[...], wb_l[...], envelope * (silu0[:, here] + value))
        lower[:, here] = after[:width]
        small[ep1, here] = after[width:]
        scatter(times3(unit, after[width:]), here)

    env1 = loop(phase_b)

    def phase_c(here, i):
        envelope = geo[3:4, here]
        at_pairs = gather(env1, here)
        vectors = v1s[:, here]
        update = lower[:, here] + dot(s1[...], stack3(fold3(vectors * at_pairs)))
        value, deriv = silu_pair(update)
        weight = energy_rows()
        geo[6:7, here] = jnp.sum(weight * value, axis=0, keepdims=True)
        back = mul3(t1_h[...], t1_l[...], weight * deriv * envelope)
        dlat[:, here] = weight + back[:width]
        d_scalar = tile3(back[width:])
        dv1s[:, here] = d_scalar * at_pairs
        scatter(d_scalar * vectors, here)

    denv1 = loop(phase_c)

    def phase_d(here, i):
        unit, envelope = geo[0:3, here], geo[3:4, here]
        d_spread = gather(denv1, here)
        d_unit = sums3(d_spread * tile3(small[ep1, here]))
        at_pairs = at0s[:, here]
        dv1 = dv1s[:, here]
        d_latent = dlat[:, here] + dot(e1_t[...], stack3(sum3(d_spread, unit)))
        d_gate = fold3(dv1 * at_pairs)
        back = mul3(t0_h[...], t0_l[...], d_latent * envelope * dsilu1[:, here])
        geo[6:7, here] = geo[6:7, here] + jnp.sum(d_latent * silu1[:, here], axis=0, keepdims=True)
        dlat[:, here] = d_latent + back[:width] + dot(gate_t[...], stack3(d_gate))
        d_scalar = back[width:]
        vw_here = small[vw, here]
        d_vectors = dv1 + tile3(d_scalar) * at_pairs
        small[dvw, here] = sum3(d_vectors, unit)
        geo[8:11, here] = d_unit + sums3(d_vectors * tile3(vw_here))
        scatter(dv1 * tile3(small[g0, here]) + times3(unit, d_scalar * vw_here), here)

    denv0 = loop(phase_d)

    def phase_e(here, i):
        unit, envelope = geo[0:3, here], geo[3:4, here]
        d_spread = gather(denv0, here)
        d_unit = geo[8:11, here] + sums3(d_spread * tile3(small[ep0, here]))
        d_latent = dlat[:, here] + dot(e0_t[...], stack3(sum3(d_spread, unit)))
        d_vw = small[dvw, here]
        d_envelope = (
            geo[6:7, here]
            + jnp.sum(d_latent * silu0[:, here], axis=0, keepdims=True)
            + jnp.sum(d_vw * small[vb, here], axis=0, keepdims=True)
        )
        d_first = jnp.concatenate(
            [d_latent * envelope * dsilu0[:, here], tall(envelope * d_vw, 128)], axis=0
        )
        d_bases[0:8, here] = mul3(back_h[...], back_l[...], d_first)[:8]
        geo[6:7, here] = d_envelope
        geo[8:11, here] = d_unit

    lax.fori_loop(0, steps, lambda i, c: (phase_e(at(i), i), c)[1], 0)
    unit, d_unit = geo[0:3], geo[8:11]
    d_distance = jnp.sum(d_bases[...] * trig[...], axis=0, keepdims=True) + geo[6:7] * geo[5:6]
    along = jnp.sum(unit * d_unit, axis=0, keepdims=True)
    d_move = unit * d_distance + (d_unit - unit * along) * geo[4:5]
    high, low = split(tall(d_move, 16))
    by_centre = dot_t(jnp.concatenate([high, low], axis=0), mem_t[...])
    high, low = split(
        jnp.concatenate([jnp.where(hot, d_move[m : m + 1], 0.0) for m in range(3)], axis=0)
    )
    by_slot = dot_t(jnp.concatenate([high, low], axis=0), nbr_t[...])
    return by_slot[:96] + by_slot[96:], by_centre[:16] + by_centre[16:]


def weight_scratch(width, ch):
    def b(*shape):
        return pltpu.VMEM(shape, BF16)

    return [
        b(width + 128, 128),
        b(width + 2 * ch, width),
        b(width + 2 * ch, width),
        b(width + ch, width),
        b(width + ch, width),
        b(width, 128),
        b(width, 128),
        b(width + ch, width),
        b(width + ch, width),
        b(width + ch, width),
        b(width + ch, width),
        b(width, 128),
        b(width, 128),
        b(width, 128),
        b(16, width + 128),
        b(16, width + 128),
        pltpu.VMEM((width, 128), F32),
    ]


def store_scratch(width, ch, count, atoms):
    def f(*shape):
        return pltpu.VMEM(shape, F32)

    return [
        f(16, count),
        f(8, count),
        f(width, count),
        f(width, count),
        f(width, count),
        f(width, count),
        f(width, count),
        f(width, count),
        f(6 * ch, count),
        f(3 * ch, count),
        f(3 * ch, count),
        f(3 * ch, count),
        f(width, count),
        f(6 * ch, atoms),
        pltpu.VMEM((128, count), BF16),
        f(8, count),
    ]


def wrapped(step, size):
    return step % size


def kernel(
    sizes,
    live_ref,
    owner_ref,
    pos,
    vel,
    kind,
    pair,
    radial,
    centre_e,
    neigh_e,
    vector,
    env_w,
    gate_w,
    latent_w,
    energy,
    out,
    *scratch,
):
    xs, ys, zs = sizes
    weights = scratch[47:]
    w_scratch, store = scratch[:17], scratch[17:33]
    (mem_t, nbr_t, halo, force_out, force_in, move_out, move_in,
     pos_send, pos_recv, force_send, force_recv, move_send, move_recv, load_sem) = scratch[33:47]
    loads = [
        pltpu.make_async_copy(source, target, load_sem.at[k])
        for k, (source, target) in enumerate(
            zip((radial, centre_e, neigh_e, vector, env_w, gate_w, latent_w, energy), weights)
        )
    ]
    for load in loads:
        load.start()
    atoms = vel.shape[2]
    me = (lax.axis_index("gx"), lax.axis_index("gy"), lax.axis_index("gz"))

    def device(step):
        return tuple(lax.rem(m + s % n, n) for m, s, n in zip(me, step, sizes))

    slots = [(x, y, z) for x in (-1, 0, 1) for y in (-1, 0, 1) for z in (-1, 0, 1)]
    first = {}
    for k, s in enumerate(slots):
        first.setdefault((s[0] % xs, s[1] % ys, s[2] % zs), k)
    leader = [first[(s[0] % xs, s[1] % ys, s[2] % zs)] for s in slots]
    home = first[(0, 0, 0)]
    leaders = [k for k in first.values() if k != home]
    partners = {(s[0] % xs, s[1] % ys, s[2] % zs) for s in (slots[k] for k in leaders)}
    partners |= {((-x) % xs, (-y) % ys, (-z) % zs) for x, y, z in partners}
    partners |= {(0, 0, z) for z in range(1, zs)}
    partners = sorted(partners)

    barrier = pltpu.get_barrier_semaphore()
    for step in partners:
        pl.semaphore_signal(barrier, inc=1, device_id=device(step), device_id_type=MESH)
    here = jnp.concatenate([pos[0, :, m * atoms : (m + 1) * atoms] for m in range(3)], axis=0)
    pl.semaphore_wait(barrier, len(partners))

    def push(k, source, target, send, recv, step):
        return pltpu.make_async_remote_copy(
            src_ref=source, dst_ref=target, send_sem=send.at[k], recv_sem=recv.at[k],
            device_id=device(step), device_id_type=MESH,
        )

    pos_copies = [
        push(k, pos.at[0], halo.at[k], pos_send, pos_recv, tuple(-v for v in slots[k])) for k in leaders
    ]
    for copy in pos_copies:
        copy.start()

    hot_matrices(pair, mem_t, nbr_t, atoms)
    species_hot = (
        lax.broadcasted_iota(jnp.int32, (8, atoms), 0) == kind[...]
    ).astype(F32)
    high, mid, low = (v.astype(F32) for v in split3(tall(here, 8)))
    near = dot(jnp.concatenate([high, mid, low, species_hot], axis=0).astype(BF16), mem_t[...])
    near = jnp.concatenate([near[0:8] + near[8:16] + near[16:24], near[24:32]], axis=0)
    for load in loads:
        load.wait()
    prepare(weights, w_scratch)

    for copy in pos_copies:
        copy.wait()
    rows = []
    for m in range(3):
        cut = slice(m * atoms, (m + 1) * atoms)
        for k in range(SLOTS):
            rows.append(pos[0, :, cut] if leader[k] == home else halo[leader[k], :, cut])
        rows.append(jnp.zeros((32 - SLOTS, atoms), F32))
    table = jnp.concatenate(split3(jnp.concatenate(rows, axis=0)), axis=0)

    by_slot, by_centre = gradient(
        table, near, pair, live_ref[0], w_scratch, (mem_t, nbr_t), store
    )

    members = {k: [j for j in range(SLOTS) if leader[j] == k] for k in leaders + [home]}

    def piece(k):
        parts = []
        for m in range(3):
            row = by_slot[32 * m + k : 32 * m + k + 1]
            for j in members[k][1:]:
                row = row + by_slot[32 * m + j : 32 * m + j + 1]
            parts.append(row)
        return parts

    force_copies = []
    for k in leaders:
        for m, row in enumerate(piece(k)):
            force_out[k, :, m * atoms : (m + 1) * atoms] = row
        copy = push(k, force_out.at[k], force_in.at[k], force_send, force_recv, slots[k])
        copy.start()
        force_copies.append(copy)
    total = jnp.concatenate(piece(home), axis=0) - by_centre[0:3]
    inverse_mass = 1.0 / (1.0 + kind[...].astype(F32))
    velocity = jnp.concatenate([vel[0], vel[1], vel[2]], axis=0)
    for copy in force_copies:
        copy.wait()
    arrived = force_in[leaders[0]]
    for k in leaders[1:]:
        arrived = arrived + force_in[k]
    total = total + jnp.concatenate(
        [arrived[:, m * atoms : (m + 1) * atoms] for m in range(3)], axis=0
    )
    forces = -total
    new_vel = velocity + TIME_STEP * forces * inverse_mass
    new_pos = here + TIME_STEP * new_vel
    state = jnp.concatenate([new_pos, new_vel, forces], axis=0)
    blocks = atoms // 128
    depth = float(atoms // 64)
    is_z = (lax.broadcasted_iota(jnp.int32, (9, 128), 0) == 2).astype(F32)

    def block_for(target):
        result = jnp.zeros((9, 128), F32)
        lift = (me[2] - target).astype(F32) * depth
        for b in range(blocks):
            mine = jnp.full((9, 128), owner_ref[b], jnp.int32) == target
            result = result + jnp.where(mine, state[:, 128 * b : 128 * b + 128] + is_z * lift, 0.0)
        return result

    move_copies = []
    for z in range(1, zs):
        target = lax.rem(me[2] + z, zs)
        move_out[z] = block_for(target)
        copy = push(z, move_out.at[z], move_in.at[z], move_send, move_recv, (0, 0, z))
        copy.start()
        move_copies.append(copy)
    out[me[2]] = block_for(me[2])
    for copy in move_copies:
        copy.wait()
    for z in range(1, zs):
        source = lax.rem(me[2] + zs - z, zs)
        out[source] = move_in[z]


def per_device(
    sizes,
    positions,
    velocities,
    species,
    pair_table,
    live_blocks,
    owners,
    radial_weight,
    center_embed,
    neighbour_embed,
    vector_weight,
    env_weight,
    vector_gate,
    latent_weight,
    energy_weight,
):
    atoms = positions.shape[4]
    count = pair_table.shape[4]
    width = latent_weight.shape[1]
    ch = vector_weight.shape[0]
    zs = sizes[2]
    smem = pl.BlockSpec(memory_space=pltpu.SMEM)
    vmem = pl.BlockSpec(memory_space=pltpu.VMEM)
    dma = pltpu.SemaphoreType.DMA
    weights = (
        radial_weight.T,
        center_embed.T,
        neighbour_embed.T,
        vector_weight.T,
        env_weight,
        vector_gate,
        jnp.swapaxes(latent_weight, 1, 2),
        energy_weight.reshape(1, width),
    )
    result = pl.pallas_call(
        functools.partial(kernel, sizes),
        out_shape=jax.ShapeDtypeStruct((zs, 9, 128), F32),
        in_specs=[smem, smem] + [vmem] * 4 + [pl.BlockSpec(memory_space=pl.ANY)] * 8,
        out_specs=vmem,
        scratch_shapes=weight_scratch(width, ch)
        + store_scratch(width, ch, count, atoms)
        + [
            pltpu.VMEM((atoms, count), BF16),
            pltpu.VMEM((atoms, count), BF16),
            pltpu.VMEM((SLOTS, 1, 3 * atoms), F32),
            pltpu.VMEM((SLOTS, 1, 3 * atoms), F32),
            pltpu.VMEM((SLOTS, 1, 3 * atoms), F32),
            pltpu.VMEM((zs, 9, 128), F32),
            pltpu.VMEM((zs, 9, 128), F32),
            dma((SLOTS,)),
            dma((SLOTS,)),
            dma((SLOTS,)),
            dma((SLOTS,)),
            dma((zs,)),
            dma((zs,)),
            dma((8,)),
        ]
        + [pltpu.VMEM(w.shape, F32) for w in weights],
        compiler_params=pltpu.CompilerParams(
            collective_id=0, has_side_effects=True, vmem_limit_bytes=48 << 20
        ),
    )(
        live_blocks.reshape(1),
        owners.reshape(-1),
        positions.reshape(1, 1, 3 * atoms),
        velocities.reshape(3, 1, atoms),
        species.reshape(1, atoms),
        pair_table.reshape(3, 1, count),
        *weights,
    )
    return result[None, None, None]


def solution(mesh):
    sizes = (mesh.shape["gx"], mesh.shape["gy"], mesh.shape["gz"])
    spread = ("gx", "gy", "gz")
    in_specs = (
        P(*spread, None, None),
        P(*spread, None, None),
        P(*spread, None),
        P(*spread, None, None),
        P(*spread),
        P(*spread, None),
    ) + (P(),) * 8
    return jax.shard_map(
        functools.partial(per_device, sizes),
        mesh=mesh,
        in_specs=in_specs,
        out_specs=P(*spread, None, None, None),
        check_vma=False,
    )
```

```python
import functools

import jax
import jax.numpy as jnp
from jax import lax
from jax.experimental import pallas as pl
from jax.experimental.pallas import tpu as pltpu
from jax.sharding import PartitionSpec as P

CUTOFF = 5.0
ENV_SCALE = 0.4
TIME_STEP = 0.2
CHUNK = 768
SLOTS = 27
F32 = jnp.float32
BF16 = jnp.bfloat16
MESH = pl.DeviceIdType.MESH


def split(x):
    high = x.astype(BF16)
    return high, (x - high.astype(F32)).astype(BF16)


def split3(x):
    high = x.astype(BF16)
    rest = x - high.astype(F32)
    mid = rest.astype(BF16)
    return high, mid, (rest - mid.astype(F32)).astype(BF16)


def dot(a, b):
    return jnp.dot(a, b, preferred_element_type=F32)


def dot_t(a, b):
    return lax.dot_general(a, b, (((1,), (1,)), ((), ())), preferred_element_type=F32)


def mul3(w_high, w_low, x):
    high, low = split(x)
    return dot(w_high, high) + dot(w_high, low) + dot(w_low, high)


def wide(x, lanes):
    if x.shape[1] == lanes:
        return x
    return jnp.concatenate([x, jnp.zeros((x.shape[0], lanes - x.shape[1]), x.dtype)], axis=1)


def tall(x, rows):
    if x.shape[0] == rows:
        return x
    return jnp.concatenate([x, jnp.zeros((rows - x.shape[0], x.shape[1]), x.dtype)], axis=0)


def stack3(x):
    high, low = split(x)
    rows = 3 * x.shape[0]
    pad = -rows % 128
    parts = [high.astype(F32), low.astype(F32), high.astype(F32)]
    if pad:
        parts.append(jnp.zeros((pad, x.shape[1]), F32))
    return jnp.concatenate(parts, axis=0).astype(BF16)


def pack3(transposed):
    high, low = split(transposed)
    high, low = high.astype(F32), low.astype(F32)
    rows = 3 * transposed.shape[0]
    stacked = tall(jnp.concatenate([high, high, low], axis=0), rows + (-rows % 128))
    return stacked.T.astype(BF16)


def silu_pair(x):
    gate = 0.5 + 0.5 * jnp.tanh(0.5 * x)
    value = x * gate
    return value, gate + value * (1.0 - gate)


def rows3(x):
    n = x.shape[0] // 3
    return x[:n], x[n : 2 * n], x[2 * n :]


def prepare(weights, scratch):
    radial, centre_e, neigh_e, vector, env_w, gate_w, latent_w, energy = weights
    (w_first, wa_h, wa_l, wb_h, wb_l, s0, s1, t0_h, t0_l, t1_h, t1_l, gate_t, e0_t, e1_t, back_h, back_l, ew) = scratch
    width = radial.shape[1]
    channels = vector.shape[1]
    radial_t = radial[...]
    centre_t = tall(centre_e[...], 8)
    neigh_t = tall(neigh_e[...], 8)
    vector_t = vector[...]
    zeros = jnp.zeros((8, 128), F32)
    vector_tp = wide(vector_t, 128)
    first_t = jnp.concatenate(
        [
            jnp.concatenate([radial_t, vector_tp], axis=1),
            jnp.concatenate([centre_t, zeros], axis=1),
            jnp.concatenate([neigh_t, zeros], axis=1),
        ],
        axis=0,
    )
    w_first[...] = pack3(first_t)
    layer0, layer1 = latent_w[0], latent_w[1]
    high, low = split(jnp.concatenate([layer0[:width].T, gate_w[...], env_w[0]], axis=0))
    wa_h[...], wa_l[...] = high, low
    high, low = split(jnp.concatenate([layer1[:width].T, env_w[1]], axis=0))
    wb_h[...], wb_l[...] = high, low
    s0[...] = pack3(layer0[width : width + channels])
    s1[...] = pack3(layer1[width : width + channels])
    t0_h[...], t0_l[...] = split(layer0)
    t1_h[...], t1_l[...] = split(layer1)
    gate_t[...] = pack3(gate_w[...])
    e0_t[...] = pack3(env_w[0])
    e1_t[...] = pack3(env_w[1])
    back = tall(jnp.concatenate([radial_t, vector_tp], axis=1), 16)
    back_h[...], back_l[...] = split(back)
    ew[...] = jnp.broadcast_to(tall(energy[...], 8).T[:, :1], (width, 128))


def hot_matrices(pair, mem_t, nbr_t, atoms):
    count = pair.shape[2]
    labels = lax.broadcasted_iota(jnp.int32, (atoms, CHUNK), 0)

    def chunk(i, carry):
        here = pl.ds(pl.multiple_of(i * CHUNK, CHUNK), CHUNK)
        centre = pair[0, :, here]
        atom = pair[1, :, here] & (atoms - 1)
        mem_t[:, here] = (labels == centre).astype(F32).astype(BF16)
        nbr_t[:, here] = (labels == atom).astype(F32).astype(BF16)
        return carry

    lax.fori_loop(0, count // CHUNK, chunk, 0)


def sum3(values, by):
    a, b, c = rows3(values)
    return a * by[0:1] + b * by[1:2] + c * by[2:3]


def times3(by, value):
    return jnp.concatenate([value * by[0:1], value * by[1:2], value * by[2:3]], axis=0)


def tile3(value):
    return jnp.concatenate([value, value, value], axis=0)


def fold3(values):
    a, b, c = rows3(values)
    return a + b + c


def sums3(values):
    a, b, c = rows3(values)
    return jnp.concatenate(
        [jnp.sum(a, axis=0, keepdims=True), jnp.sum(b, axis=0, keepdims=True), jnp.sum(c, axis=0, keepdims=True)],
        axis=0,
    )


def gradient(table, near, pair, live, weights, hots, store):
    (w_first, wa_h, wa_l, wb_h, wb_l, s0, s1, t0_h, t0_l, t1_h, t1_l, gate_t, e0_t, e1_t, back_h, back_l, ew) = weights
    mem_t, nbr_t = hots
    (geo, trig, silu0, dsilu0, upper, lower, silu1, dsilu1, small, at0s, v1s, dv1s, dlat, acc, firsts, d_bases) = store
    atoms, count = mem_t.shape
    depth = float(atoms // 64)
    width = silu0.shape[0]
    ch = v1s.shape[0] // 3
    steps = count // CHUNK
    vw, vb, g0, ep0, ep1, dvw = (slice(k * ch, (k + 1) * ch) for k in range(6))

    def at(i):
        return pl.ds(pl.multiple_of(i * CHUNK, CHUNK), CHUNK)

    def loop(body):
        acc[...] = jnp.zeros_like(acc)
        lax.fori_loop(0, steps, lambda i, c: (body(at(i), i), c)[1], 0)
        total = acc[...]
        n = total.shape[0] // 2
        high, low = split(ENV_SCALE * (total[:n] + total[n:]))
        return jnp.concatenate([high, low], axis=0)

    def gather(two, here):
        both = dot(two, mem_t[:, here])
        n = both.shape[0] // 2
        return both[:n] + both[n:]

    def scatter(values, here):
        high, low = split(values)
        acc[...] += dot_t(jnp.concatenate([high, low], axis=0), mem_t[:, here])

    def energy_rows():
        value = ew[...]
        return jnp.concatenate([value] * (CHUNK // 128), axis=1)

    slot = pair[1] // atoms
    hot = lax.broadcasted_iota(jnp.int32, (32, count), 0) == slot
    far = dot(table, nbr_t[...])
    far = far[:96] + far[96:192] + far[192:]
    picks = [jnp.sum(jnp.where(hot, far[32 * m : 32 * m + 32], 0.0), axis=0, keepdims=True) for m in range(3)]
    dx = picks[0] + (slot // 9 - 1).astype(F32) * 8.0 - near[0:1]
    dy = picks[1] + (slot // 3 % 3 - 1).astype(F32) * 8.0 - near[1:2]
    dz = picks[2] + (slot % 3 - 1).astype(F32) * depth - near[2:3]
    distance = jnp.sqrt(dx * dx + dy * dy + dz * dz)
    inverse = 1.0 / distance
    ratio = distance / CUTOFF
    lanes = lax.broadcasted_iota(jnp.int32, (1, count), 1)
    use = (lanes < live * 128).astype(F32)
    bump = 1.0 - ratio * ratio
    geo[0:3] = jnp.concatenate([dx, dy, dz], axis=0) * inverse
    geo[3:4] = bump * bump * use
    geo[4:5] = inverse
    geo[5:6] = bump * use * (-4.0 / CUTOFF) * ratio
    orders = (lax.broadcasted_iota(jnp.int32, (8, count), 0) + 1).astype(F32)
    angle = orders * jnp.pi * distance / CUTOFF
    norm = (2.0 / CUTOFF) ** 0.5 * inverse
    basis = norm * jnp.sin(angle)
    trig[...] = norm * (orders * (jnp.pi / CUTOFF)) * jnp.cos(angle) - basis * inverse
    other_hot = (lax.broadcasted_iota(jnp.int32, (8, count), 0) == pair[2]).astype(F32)
    firsts[...] = stack3(jnp.concatenate([basis, near[8:16], other_hot], axis=0))

    def phase_a(here, i):
        unit, envelope = geo[0:3, here], geo[3:4, here]
        first = dot(w_first[...], firsts[:, here])
        value, deriv = silu_pair(first[:width])
        silu0[:, here] = value
        dsilu0[:, here] = deriv
        plain = first[width : width + ch]
        small[vb, here] = plain
        small[vw, here] = envelope * plain
        after = mul3(wa_h[...], wa_l[...], envelope * value)
        upper[:, here] = after[:width]
        small[g0, here] = after[width : width + ch]
        small[ep0, here] = after[width + ch :]
        scatter(times3(unit, after[width + ch :]), here)

    env0 = loop(phase_a)

    def phase_b(here, i):
        unit, envelope = geo[0:3, here], geo[3:4, here]
        at_pairs = gather(env0, here)
        at0s[:, here] = at_pairs
        vw_here = small[vw, here]
        scalars = vw_here * sum3(at_pairs, unit)
        update = upper[:, here] + dot(s0[...], stack3(scalars))
        value, deriv = silu_pair(update)
        silu1[:, here] = value
        dsilu1[:, here] = deriv
        v1s[:, here] = times3(unit, vw_here) + at_pairs * tile3(small[g0, here])
        after = mul3(wb_h[...], wb_l[...], envelope * (silu0[:, here] + value))
        lower[:, here] = after[:width]
        small[ep1, here] = after[width:]
        scatter(times3(unit, after[width:]), here)

    env1 = loop(phase_b)

    def phase_c(here, i):
        envelope = geo[3:4, here]
        at_pairs = gather(env1, here)
        vectors = v1s[:, here]
        update = lower[:, here] + dot(s1[...], stack3(fold3(vectors * at_pairs)))
        value, deriv = silu_pair(update)
        weight = energy_rows()
        geo[6:7, here] = jnp.sum(weight * value, axis=0, keepdims=True)
        back = mul3(t1_h[...], t1_l[...], weight * deriv * envelope)
        dlat[:, here] = weight + back[:width]
        d_scalar = tile3(back[width:])
        dv1s[:, here] = d_scalar * at_pairs
        scatter(d_scalar * vectors, here)

    denv1 = loop(phase_c)

    def phase_d(here, i):
        unit, envelope = geo[0:3, here], geo[3:4, here]
        d_spread = gather(denv1, here)
        d_unit = sums3(d_spread * tile3(small[ep1, here]))
        at_pairs = at0s[:, here]
        dv1 = dv1s[:, here]
        d_latent = dlat[:, here] + dot(e1_t[...], stack3(sum3(d_spread, unit)))
        d_gate = fold3(dv1 * at_pairs)
        back = mul3(t0_h[...], t0_l[...], d_latent * envelope * dsilu1[:, here])
        geo[6:7, here] = geo[6:7, here] + jnp.sum(d_latent * silu1[:, here], axis=0, keepdims=True)
        dlat[:, here] = d_latent + back[:width] + dot(gate_t[...], stack3(d_gate))
        d_scalar = back[width:]
        vw_here = small[vw, here]
        d_vectors = dv1 + tile3(d_scalar) * at_pairs
        small[dvw, here] = sum3(d_vectors, unit)
        geo[8:11, here] = d_unit + sums3(d_vectors * tile3(vw_here))
        scatter(dv1 * tile3(small[g0, here]) + times3(unit, d_scalar * vw_here), here)

    denv0 = loop(phase_d)

    def phase_e(here, i):
        unit, envelope = geo[0:3, here], geo[3:4, here]
        d_spread = gather(denv0, here)
        d_unit = geo[8:11, here] + sums3(d_spread * tile3(small[ep0, here]))
        d_latent = dlat[:, here] + dot(e0_t[...], stack3(sum3(d_spread, unit)))
        d_vw = small[dvw, here]
        d_envelope = (
            geo[6:7, here]
            + jnp.sum(d_latent * silu0[:, here], axis=0, keepdims=True)
            + jnp.sum(d_vw * small[vb, here], axis=0, keepdims=True)
        )
        d_first = jnp.concatenate(
            [d_latent * envelope * dsilu0[:, here], tall(envelope * d_vw, 128)], axis=0
        )
        d_bases[0:8, here] = mul3(back_h[...], back_l[...], d_first)[:8]
        geo[6:7, here] = d_envelope
        geo[8:11, here] = d_unit

    lax.fori_loop(0, steps, lambda i, c: (phase_e(at(i), i), c)[1], 0)
    unit, d_unit = geo[0:3], geo[8:11]
    d_distance = jnp.sum(d_bases[...] * trig[...], axis=0, keepdims=True) + geo[6:7] * geo[5:6]
    along = jnp.sum(unit * d_unit, axis=0, keepdims=True)
    d_move = unit * d_distance + (d_unit - unit * along) * geo[4:5]
    high, low = split(tall(d_move, 16))
    by_centre = dot_t(jnp.concatenate([high, low], axis=0), mem_t[...])
    high, low = split(
        jnp.concatenate([jnp.where(hot, d_move[m : m + 1], 0.0) for m in range(3)], axis=0)
    )
    by_slot = dot_t(jnp.concatenate([high, low], axis=0), nbr_t[...])
    return by_slot[:96] + by_slot[96:], by_centre[:16] + by_centre[16:]


def weight_scratch(width, ch):
    def b(*shape):
        return pltpu.VMEM(shape, BF16)

    return [
        b(width + 128, 128),
        b(width + 2 * ch, width),
        b(width + 2 * ch, width),
        b(width + ch, width),
        b(width + ch, width),
        b(width, 128),
        b(width, 128),
        b(width + ch, width),
        b(width + ch, width),
        b(width + ch, width),
        b(width + ch, width),
        b(width, 128),
        b(width, 128),
        b(width, 128),
        b(16, width + 128),
        b(16, width + 128),
        pltpu.VMEM((width, 128), F32),
    ]


def store_scratch(width, ch, count, atoms):
    def f(*shape):
        return pltpu.VMEM(shape, F32)

    return [
        f(16, count),
        f(8, count),
        f(width, count),
        f(width, count),
        f(width, count),
        f(width, count),
        f(width, count),
        f(width, count),
        f(6 * ch, count),
        f(3 * ch, count),
        f(3 * ch, count),
        f(3 * ch, count),
        f(width, count),
        f(6 * ch, atoms),
        pltpu.VMEM((128, count), BF16),
        f(8, count),
    ]


def wrapped(step, size):
    return step % size


def kernel(
    sizes,
    *refs,
):
    xs, ys, zs = sizes
    sources, out, scratch = refs[:14], refs[14], refs[15:]
    loaded = scratch[47:]
    pair, kind, pos, live_ref, vel, owner_ref = loaded[:6]
    weights = loaded[6:]
    w_scratch, store = scratch[:17], scratch[17:33]
    (mem_t, nbr_t, halo, force_out, force_in, move_out, move_in,
     pos_send, pos_recv, force_send, force_recv, move_send, move_recv, load_sem) = scratch[33:47]
    loads = [
        pltpu.make_async_copy(source, target, load_sem.at[k])
        for k, (source, target) in enumerate(zip(sources, loaded))
    ]
    for load in loads:
        load.start()
    atoms = vel.shape[2]
    me = (lax.axis_index("gx"), lax.axis_index("gy"), lax.axis_index("gz"))

    def device(step):
        return tuple(lax.rem(m + s % n, n) for m, s, n in zip(me, step, sizes))

    slots = [(x, y, z) for x in (-1, 0, 1) for y in (-1, 0, 1) for z in (-1, 0, 1)]
    first = {}
    for k, s in enumerate(slots):
        first.setdefault((s[0] % xs, s[1] % ys, s[2] % zs), k)
    leader = [first[(s[0] % xs, s[1] % ys, s[2] % zs)] for s in slots]
    home = first[(0, 0, 0)]
    leaders = [k for k in first.values() if k != home]
    partners = {(s[0] % xs, s[1] % ys, s[2] % zs) for s in (slots[k] for k in leaders)}
    partners |= {((-x) % xs, (-y) % ys, (-z) % zs) for x, y, z in partners}
    partners |= {(0, 0, z) for z in range(1, zs)}
    partners = sorted(partners)

    barrier = pltpu.get_barrier_semaphore()
    for step in partners:
        pl.semaphore_signal(barrier, inc=1, device_id=device(step), device_id_type=MESH)
    pl.semaphore_wait(barrier, len(partners))

    def push(k, source, target, send, recv, step):
        return pltpu.make_async_remote_copy(
            src_ref=source, dst_ref=target, send_sem=send.at[k], recv_sem=recv.at[k],
            device_id=device(step), device_id_type=MESH,
        )

    pos_copies = [
        push(k, sources[2].at[0], halo.at[k], pos_send, pos_recv, tuple(-v for v in slots[k])) for k in leaders
    ]
    for copy in pos_copies:
        copy.start()

    for load in loads[:3]:
        load.wait()
    hot_matrices(pair, mem_t, nbr_t, atoms)
    here = jnp.concatenate([pos[0, :, m * atoms : (m + 1) * atoms] for m in range(3)], axis=0)
    species_hot = (
        lax.broadcasted_iota(jnp.int32, (8, atoms), 0) == kind[...]
    ).astype(F32)
    high, mid, low = (v.astype(F32) for v in split3(tall(here, 8)))
    near = dot(jnp.concatenate([high, mid, low, species_hot], axis=0).astype(BF16), mem_t[...])
    near = jnp.concatenate([near[0:8] + near[8:16] + near[16:24], near[24:32]], axis=0)
    for load in loads[3:]:
        load.wait()
    prepare(weights, w_scratch)

    for copy in pos_copies:
        copy.wait()
    rows = []
    for m in range(3):
        cut = slice(m * atoms, (m + 1) * atoms)
        for k in range(SLOTS):
            rows.append(pos[0, :, cut] if leader[k] == home else halo[leader[k], :, cut])
        rows.append(jnp.zeros((32 - SLOTS, atoms), F32))
    table = jnp.concatenate(split3(jnp.concatenate(rows, axis=0)), axis=0)

    by_slot, by_centre = gradient(
        table, near, pair, live_ref[...], w_scratch, (mem_t, nbr_t), store
    )

    members = {k: [j for j in range(SLOTS) if leader[j] == k] for k in leaders + [home]}

    def piece(k):
        parts = []
        for m in range(3):
            row = by_slot[32 * m + k : 32 * m + k + 1]
            for j in members[k][1:]:
                row = row + by_slot[32 * m + j : 32 * m + j + 1]
            parts.append(row)
        return parts

    force_copies = []
    for k in leaders:
        for m, row in enumerate(piece(k)):
            force_out[k, :, m * atoms : (m + 1) * atoms] = row
        copy = push(k, force_out.at[k], force_in.at[k], force_send, force_recv, slots[k])
        copy.start()
        force_copies.append(copy)
    total = jnp.concatenate(piece(home), axis=0) - by_centre[0:3]
    inverse_mass = 1.0 / (1.0 + kind[...].astype(F32))
    velocity = jnp.concatenate([vel[0], vel[1], vel[2]], axis=0)
    for copy in force_copies:
        copy.wait()
    arrived = force_in[leaders[0]]
    for k in leaders[1:]:
        arrived = arrived + force_in[k]
    total = total + jnp.concatenate(
        [arrived[:, m * atoms : (m + 1) * atoms] for m in range(3)], axis=0
    )
    forces = -total
    new_vel = velocity + TIME_STEP * forces * inverse_mass
    new_pos = here + TIME_STEP * new_vel
    state = jnp.concatenate([new_pos, new_vel, forces], axis=0)
    blocks = atoms // 128
    depth = float(atoms // 64)
    is_z = (lax.broadcasted_iota(jnp.int32, (9, 128), 0) == 2).astype(F32)

    def block_for(target):
        result = jnp.zeros((9, 128), F32)
        lift = (me[2] - target).astype(F32) * depth
        for b in range(blocks):
            mine = jnp.broadcast_to(owner_ref[:, b : b + 1], (9, 128)) == target
            result = result + jnp.where(mine, state[:, 128 * b : 128 * b + 128] + is_z * lift, 0.0)
        return result

    move_copies = []
    for z in range(1, zs):
        target = lax.rem(me[2] + z, zs)
        move_out[z] = block_for(target)
        copy = push(z, move_out.at[z], move_in.at[z], move_send, move_recv, (0, 0, z))
        copy.start()
        move_copies.append(copy)
    out[me[2]] = block_for(me[2])
    for copy in move_copies:
        copy.wait()
    for z in range(1, zs):
        source = lax.rem(me[2] + zs - z, zs)
        out[source] = move_in[z]


def per_device(
    sizes,
    positions,
    velocities,
    species,
    pair_table,
    live_blocks,
    owners,
    radial_weight,
    center_embed,
    neighbour_embed,
    vector_weight,
    env_weight,
    vector_gate,
    latent_weight,
    energy_weight,
):
    atoms = positions.shape[4]
    count = pair_table.shape[4]
    width = latent_weight.shape[1]
    ch = vector_weight.shape[0]
    zs = sizes[2]
    dma = pltpu.SemaphoreType.DMA
    operands = (
        pair_table.reshape(3, 1, count),
        species.reshape(1, atoms),
        positions.reshape(1, 1, 3 * atoms),
        live_blocks.reshape(1, 1),
        velocities.reshape(3, 1, atoms),
        owners.reshape(1, -1),
        radial_weight.T,
        center_embed.T,
        neighbour_embed.T,
        vector_weight.T,
        env_weight,
        vector_gate,
        jnp.swapaxes(latent_weight, 1, 2),
        energy_weight.reshape(1, width),
    )
    result = pl.pallas_call(
        functools.partial(kernel, sizes),
        out_shape=jax.ShapeDtypeStruct((zs, 9, 128), F32),
        in_specs=[pl.BlockSpec(memory_space=pl.ANY)] * 14,
        out_specs=pl.BlockSpec(memory_space=pltpu.VMEM),
        scratch_shapes=weight_scratch(width, ch)
        + store_scratch(width, ch, count, atoms)
        + [
            pltpu.VMEM((atoms, count), BF16),
            pltpu.VMEM((atoms, count), BF16),
            pltpu.VMEM((SLOTS, 1, 3 * atoms), F32),
            pltpu.VMEM((SLOTS, 1, 3 * atoms), F32),
            pltpu.VMEM((SLOTS, 1, 3 * atoms), F32),
            pltpu.VMEM((zs, 9, 128), F32),
            pltpu.VMEM((zs, 9, 128), F32),
            dma((SLOTS,)),
            dma((SLOTS,)),
            dma((SLOTS,)),
            dma((SLOTS,)),
            dma((zs,)),
            dma((zs,)),
            dma((14,)),
        ]
        + [pltpu.VMEM(v.shape, v.dtype) for v in operands],
        compiler_params=pltpu.CompilerParams(
            collective_id=0, has_side_effects=True, vmem_limit_bytes=60 << 20
        ),
    )(*operands)
    return result[None, None, None]


def solution(mesh):
    sizes = (mesh.shape["gx"], mesh.shape["gy"], mesh.shape["gz"])
    spread = ("gx", "gy", "gz")
    in_specs = (
        P(*spread, None, None),
        P(*spread, None, None),
        P(*spread, None),
        P(*spread, None, None),
        P(*spread),
        P(*spread, None),
    ) + (P(),) * 8
    return jax.shard_map(
        functools.partial(per_device, sizes),
        mesh=mesh,
        in_specs=in_specs,
        out_specs=P(*spread, None, None, None),
        check_vma=False,
    )
```

```python
import functools

import jax
import jax.numpy as jnp
from jax import lax
from jax.experimental import pallas as pl
from jax.experimental.pallas import tpu as pltpu
from jax.sharding import PartitionSpec as P

CUTOFF = 5.0
ENV_SCALE = 0.4
TIME_STEP = 0.2
CHUNK = 768
SLOTS = 27
F32 = jnp.float32
BF16 = jnp.bfloat16
MESH = pl.DeviceIdType.MESH


def split(x):
    high = x.astype(BF16)
    return high, (x - high.astype(F32)).astype(BF16)


def split3(x):
    high = x.astype(BF16)
    rest = x - high.astype(F32)
    mid = rest.astype(BF16)
    return high, mid, (rest - mid.astype(F32)).astype(BF16)


def dot(a, b):
    return jnp.dot(a, b, preferred_element_type=F32)


def dot_t(a, b):
    return lax.dot_general(a, b, (((1,), (1,)), ((), ())), preferred_element_type=F32)


def mul3(w_high, w_low, x):
    high, low = split(x)
    return dot(w_high, high) + dot(w_high, low) + dot(w_low, high)


def wide(x, lanes):
    if x.shape[1] == lanes:
        return x
    return jnp.concatenate([x, jnp.zeros((x.shape[0], lanes - x.shape[1]), x.dtype)], axis=1)


def tall(x, rows):
    if x.shape[0] == rows:
        return x
    return jnp.concatenate([x, jnp.zeros((rows - x.shape[0], x.shape[1]), x.dtype)], axis=0)


def stack3(x):
    high, low = split(x)
    rows = 3 * x.shape[0]
    pad = -rows % 128
    parts = [high.astype(F32), low.astype(F32), high.astype(F32)]
    if pad:
        parts.append(jnp.zeros((pad, x.shape[1]), F32))
    return jnp.concatenate(parts, axis=0).astype(BF16)


def pack3(transposed):
    high, low = split(transposed)
    high, low = high.astype(F32), low.astype(F32)
    rows = 3 * transposed.shape[0]
    stacked = tall(jnp.concatenate([high, high, low], axis=0), rows + (-rows % 128))
    return stacked.T.astype(BF16)


def silu_pair(x):
    gate = 0.5 + 0.5 * jnp.tanh(0.5 * x)
    value = x * gate
    return value, gate + value * (1.0 - gate)


def rows3(x):
    n = x.shape[0] // 3
    return x[:n], x[n : 2 * n], x[2 * n :]


def prepare(weights, scratch):
    radial, centre_e, neigh_e, vector, env_w, gate_w, latent_w, energy = weights
    (w_first, wa_h, wa_l, wb_h, wb_l, s0, s1, t0_h, t0_l, t1_h, t1_l, gate_t, e0_t, e1_t, back_h, back_l, ew) = scratch
    width = radial.shape[1]
    channels = vector.shape[1]
    radial_t = radial[...]
    centre_t = tall(centre_e[...], 8)
    neigh_t = tall(neigh_e[...], 8)
    vector_t = vector[...]
    zeros = jnp.zeros((8, 128), F32)
    vector_tp = wide(vector_t, 128)
    first_t = jnp.concatenate(
        [
            jnp.concatenate([radial_t, vector_tp], axis=1),
            jnp.concatenate([centre_t, zeros], axis=1),
            jnp.concatenate([neigh_t, zeros], axis=1),
        ],
        axis=0,
    )
    w_first[...] = pack3(first_t)
    layer0, layer1 = latent_w[0], latent_w[1]
    high, low = split(jnp.concatenate([layer0[:width].T, gate_w[...], env_w[0]], axis=0))
    wa_h[...], wa_l[...] = high, low
    high, low = split(jnp.concatenate([layer1[:width].T, env_w[1]], axis=0))
    wb_h[...], wb_l[...] = high, low
    s0[...] = pack3(layer0[width : width + channels])
    s1[...] = pack3(layer1[width : width + channels])
    t0_h[...], t0_l[...] = split(layer0)
    t1_h[...], t1_l[...] = split(layer1)
    gate_t[...] = pack3(gate_w[...])
    e0_t[...] = pack3(env_w[0])
    e1_t[...] = pack3(env_w[1])
    back = tall(jnp.concatenate([radial_t, vector_tp], axis=1), 16)
    back_h[...], back_l[...] = split(back)
    ew[...] = jnp.broadcast_to(tall(energy[...], 8).T[:, :1], (width, 128))


def hot_matrices(pair, mem_t, nbr_t, atoms):
    count = pair.shape[2]
    labels = lax.broadcasted_iota(jnp.int32, (atoms, CHUNK), 0)

    def chunk(i, carry):
        here = pl.ds(pl.multiple_of(i * CHUNK, CHUNK), CHUNK)
        centre = pair[0, :, here]
        atom = pair[1, :, here] & (atoms - 1)
        mem_t[:, here] = (labels == centre).astype(F32).astype(BF16)
        nbr_t[:, here] = (labels == atom).astype(F32).astype(BF16)
        return carry

    lax.fori_loop(0, count // CHUNK, chunk, 0)


def sum3(values, by):
    a, b, c = rows3(values)
    return a * by[0:1] + b * by[1:2] + c * by[2:3]


def times3(by, value):
    return jnp.concatenate([value * by[0:1], value * by[1:2], value * by[2:3]], axis=0)


def tile3(value):
    return jnp.concatenate([value, value, value], axis=0)


def fold3(values):
    a, b, c = rows3(values)
    return a + b + c


def sums3(values):
    a, b, c = rows3(values)
    return jnp.concatenate(
        [jnp.sum(a, axis=0, keepdims=True), jnp.sum(b, axis=0, keepdims=True), jnp.sum(c, axis=0, keepdims=True)],
        axis=0,
    )


def gradient(table, near, pair, live, weights, hots, store):
    (w_first, wa_h, wa_l, wb_h, wb_l, s0, s1, t0_h, t0_l, t1_h, t1_l, gate_t, e0_t, e1_t, back_h, back_l, ew) = weights
    mem_t, nbr_t = hots
    (geo, trig, silu0, dsilu0, upper, lower, silu1, dsilu1, small, at0s, v1s, dv1s, dlat, acc, firsts, d_bases) = store
    atoms, count = mem_t.shape
    depth = float(atoms // 64)
    width = silu0.shape[0]
    ch = v1s.shape[0] // 3
    steps = count // CHUNK
    vw, vb, g0, ep0, ep1, dvw = (slice(k * ch, (k + 1) * ch) for k in range(6))

    def at(i):
        return pl.ds(pl.multiple_of(i * CHUNK, CHUNK), CHUNK)

    def loop(body):
        acc[...] = jnp.zeros_like(acc)
        lax.fori_loop(0, steps, lambda i, c: (body(at(i), i), c)[1], 0)
        total = acc[...]
        n = total.shape[0] // 2
        high, low = split(ENV_SCALE * (total[:n] + total[n:]))
        return jnp.concatenate([high, low], axis=0)

    def gather(two, here):
        both = dot(two, mem_t[:, here])
        n = both.shape[0] // 2
        return both[:n] + both[n:]

    def scatter(values, here):
        high, low = split(values)
        acc[...] += dot_t(jnp.concatenate([high, low], axis=0), mem_t[:, here])

    def energy_rows():
        value = ew[...]
        return jnp.concatenate([value] * (CHUNK // 128), axis=1)

    slot = pair[1] // atoms
    hot = lax.broadcasted_iota(jnp.int32, (32, count), 0) == slot
    far = dot(table, nbr_t[...])
    far = far[:96] + far[96:192] + far[192:]
    picks = [jnp.sum(jnp.where(hot, far[32 * m : 32 * m + 32], 0.0), axis=0, keepdims=True) for m in range(3)]
    dx = picks[0] + (slot // 9 - 1).astype(F32) * 8.0 - near[0:1]
    dy = picks[1] + (slot // 3 % 3 - 1).astype(F32) * 8.0 - near[1:2]
    dz = picks[2] + (slot % 3 - 1).astype(F32) * depth - near[2:3]
    distance = jnp.sqrt(dx * dx + dy * dy + dz * dz)
    inverse = 1.0 / distance
    ratio = distance / CUTOFF
    lanes = lax.broadcasted_iota(jnp.int32, (1, count), 1)
    use = (lanes < live * 128).astype(F32)
    bump = 1.0 - ratio * ratio
    geo[0:3] = jnp.concatenate([dx, dy, dz], axis=0) * inverse
    geo[3:4] = bump * bump * use
    geo[4:5] = inverse
    geo[5:6] = bump * use * (-4.0 / CUTOFF) * ratio
    orders = (lax.broadcasted_iota(jnp.int32, (8, count), 0) + 1).astype(F32)
    angle = orders * jnp.pi * distance / CUTOFF
    norm = (2.0 / CUTOFF) ** 0.5 * inverse
    basis = norm * jnp.sin(angle)
    trig[...] = norm * (orders * (jnp.pi / CUTOFF)) * jnp.cos(angle) - basis * inverse
    other_hot = (lax.broadcasted_iota(jnp.int32, (8, count), 0) == pair[2]).astype(F32)
    firsts[...] = stack3(jnp.concatenate([basis, near[8:16], other_hot], axis=0))

    def phase_a(here, i):
        unit, envelope = geo[0:3, here], geo[3:4, here]
        first = dot(w_first[...], firsts[:, here])
        value, deriv = silu_pair(first[:width])
        silu0[:, here] = value
        dsilu0[:, here] = deriv
        plain = first[width : width + ch]
        small[vb, here] = plain
        small[vw, here] = envelope * plain
        after = mul3(wa_h[...], wa_l[...], envelope * value)
        upper[:, here] = after[:width]
        small[g0, here] = after[width : width + ch]
        small[ep0, here] = after[width + ch :]
        scatter(times3(unit, after[width + ch :]), here)

    env0 = loop(phase_a)

    def phase_b(here, i):
        unit, envelope = geo[0:3, here], geo[3:4, here]
        at_pairs = gather(env0, here)
        at0s[:, here] = at_pairs
        vw_here = small[vw, here]
        scalars = vw_here * sum3(at_pairs, unit)
        update = upper[:, here] + dot(s0[...], stack3(scalars))
        value, deriv = silu_pair(update)
        silu1[:, here] = value
        dsilu1[:, here] = deriv
        v1s[:, here] = times3(unit, vw_here) + at_pairs * tile3(small[g0, here])
        after = mul3(wb_h[...], wb_l[...], envelope * (silu0[:, here] + value))
        lower[:, here] = after[:width]
        small[ep1, here] = after[width:]
        scatter(times3(unit, after[width:]), here)

    env1 = loop(phase_b)

    def phase_c(here, i):
        envelope = geo[3:4, here]
        at_pairs = gather(env1, here)
        vectors = v1s[:, here]
        update = lower[:, here] + dot(s1[...], stack3(fold3(vectors * at_pairs)))
        value, deriv = silu_pair(update)
        weight = energy_rows()
        geo[6:7, here] = jnp.sum(weight * value, axis=0, keepdims=True)
        back = mul3(t1_h[...], t1_l[...], weight * deriv * envelope)
        dlat[:, here] = weight + back[:width]
        d_scalar = tile3(back[width:])
        dv1s[:, here] = d_scalar * at_pairs
        scatter(d_scalar * vectors, here)

    denv1 = loop(phase_c)

    def phase_d(here, i):
        unit, envelope = geo[0:3, here], geo[3:4, here]
        d_spread = gather(denv1, here)
        d_unit = sums3(d_spread * tile3(small[ep1, here]))
        at_pairs = at0s[:, here]
        dv1 = dv1s[:, here]
        d_latent = dlat[:, here] + dot(e1_t[...], stack3(sum3(d_spread, unit)))
        d_gate = fold3(dv1 * at_pairs)
        back = mul3(t0_h[...], t0_l[...], d_latent * envelope * dsilu1[:, here])
        geo[6:7, here] = geo[6:7, here] + jnp.sum(d_latent * silu1[:, here], axis=0, keepdims=True)
        dlat[:, here] = d_latent + back[:width] + dot(gate_t[...], stack3(d_gate))
        d_scalar = back[width:]
        vw_here = small[vw, here]
        d_vectors = dv1 + tile3(d_scalar) * at_pairs
        small[dvw, here] = sum3(d_vectors, unit)
        geo[8:11, here] = d_unit + sums3(d_vectors * tile3(vw_here))
        scatter(dv1 * tile3(small[g0, here]) + times3(unit, d_scalar * vw_here), here)

    denv0 = loop(phase_d)

    def phase_e(here, i):
        unit, envelope = geo[0:3, here], geo[3:4, here]
        d_spread = gather(denv0, here)
        d_unit = geo[8:11, here] + sums3(d_spread * tile3(small[ep0, here]))
        d_latent = dlat[:, here] + dot(e0_t[...], stack3(sum3(d_spread, unit)))
        d_vw = small[dvw, here]
        d_envelope = (
            geo[6:7, here]
            + jnp.sum(d_latent * silu0[:, here], axis=0, keepdims=True)
            + jnp.sum(d_vw * small[vb, here], axis=0, keepdims=True)
        )
        d_first = jnp.concatenate(
            [d_latent * envelope * dsilu0[:, here], tall(envelope * d_vw, 128)], axis=0
        )
        d_bases[0:8, here] = mul3(back_h[...], back_l[...], d_first)[:8]
        geo[6:7, here] = d_envelope
        geo[8:11, here] = d_unit

    lax.fori_loop(0, steps, lambda i, c: (phase_e(at(i), i), c)[1], 0)
    unit, d_unit = geo[0:3], geo[8:11]
    d_distance = jnp.sum(d_bases[...] * trig[...], axis=0, keepdims=True) + geo[6:7] * geo[5:6]
    along = jnp.sum(unit * d_unit, axis=0, keepdims=True)
    d_move = unit * d_distance + (d_unit - unit * along) * geo[4:5]
    high, low = split(tall(d_move, 16))
    by_centre = dot_t(jnp.concatenate([high, low], axis=0), mem_t[...])
    high, low = split(
        jnp.concatenate([jnp.where(hot, d_move[m : m + 1], 0.0) for m in range(3)], axis=0)
    )
    by_slot = dot_t(jnp.concatenate([high, low], axis=0), nbr_t[...])
    return by_slot[:96] + by_slot[96:], by_centre[:16] + by_centre[16:]


def weight_scratch(width, ch):
    def b(*shape):
        return pltpu.VMEM(shape, BF16)

    return [
        b(width + 128, 128),
        b(width + 2 * ch, width),
        b(width + 2 * ch, width),
        b(width + ch, width),
        b(width + ch, width),
        b(width, 128),
        b(width, 128),
        b(width + ch, width),
        b(width + ch, width),
        b(width + ch, width),
        b(width + ch, width),
        b(width, 128),
        b(width, 128),
        b(width, 128),
        b(16, width + 128),
        b(16, width + 128),
        pltpu.VMEM((width, 128), F32),
    ]


def store_scratch(width, ch, count, atoms):
    def f(*shape):
        return pltpu.VMEM(shape, F32)

    return [
        f(16, count),
        f(8, count),
        f(width, count),
        f(width, count),
        f(width, count),
        f(width, count),
        f(width, count),
        f(width, count),
        f(6 * ch, count),
        f(3 * ch, count),
        f(3 * ch, count),
        f(3 * ch, count),
        f(width, count),
        f(6 * ch, atoms),
        pltpu.VMEM((128, count), BF16),
        f(8, count),
    ]


def wrapped(step, size):
    return step % size


def owners_of_pieces(sizes):
    xs, ys, zs = sizes
    steps = {(x % xs, y % ys, z) for x in (-1, 0, 1) for y in (-1, 0, 1) for z in range(zs)}
    return sorted(steps - {(0, 0, 0)})


def kernel(
    sizes,
    *refs,
):
    xs, ys, zs = sizes
    sources, out, scratch = refs[:14], refs[14], refs[15:]
    loaded = scratch[47:]
    pair, kind, pos, live_ref, vel, owner_ref = loaded[:6]
    weights = loaded[6:]
    w_scratch, store = scratch[:17], scratch[17:33]
    (mem_t, nbr_t, halo, force_out, force_in, info_out, info_in,
     pos_send, pos_recv, force_send, force_recv, info_send, info_recv, load_sem) = scratch[33:47]
    loads = [
        pltpu.make_async_copy(source, target, load_sem.at[k])
        for k, (source, target) in enumerate(zip(sources, loaded))
    ]
    for load in loads:
        load.start()
    atoms = vel.shape[2]
    me = (lax.axis_index("gx"), lax.axis_index("gy"), lax.axis_index("gz"))

    def device(step):
        return tuple(lax.rem(m + s % n, n) for m, s, n in zip(me, step, sizes))

    slots = [(x, y, z) for x in (-1, 0, 1) for y in (-1, 0, 1) for z in (-1, 0, 1)]
    first = {}
    for k, s in enumerate(slots):
        first.setdefault((s[0] % xs, s[1] % ys, s[2] % zs), k)
    leader = [first[(s[0] % xs, s[1] % ys, s[2] % zs)] for s in slots]
    home = first[(0, 0, 0)]
    leaders = [k for k in first.values() if k != home]
    partners = owners_of_pieces(sizes)

    barrier = pltpu.get_barrier_semaphore()
    for step in partners:
        pl.semaphore_signal(barrier, inc=1, device_id=device(step), device_id_type=MESH)
    pl.semaphore_wait(barrier, len(partners))

    def push(k, source, target, send, recv, step):
        return pltpu.make_async_remote_copy(
            src_ref=source, dst_ref=target, send_sem=send.at[k], recv_sem=recv.at[k],
            device_id=device(step), device_id_type=MESH,
        )

    pos_copies = [
        push(k, sources[2].at[0], halo.at[k], pos_send, pos_recv, tuple(-v for v in slots[k])) for k in leaders
    ]
    for copy in pos_copies:
        copy.start()

    for load in loads[:3]:
        load.wait()
    hot_matrices(pair, mem_t, nbr_t, atoms)
    here = jnp.concatenate([pos[0, :, m * atoms : (m + 1) * atoms] for m in range(3)], axis=0)
    species_hot = (
        lax.broadcasted_iota(jnp.int32, (8, atoms), 0) == kind[...]
    ).astype(F32)
    high, mid, low = (v.astype(F32) for v in split3(tall(here, 8)))
    near = dot(jnp.concatenate([high, mid, low, species_hot], axis=0).astype(BF16), mem_t[...])
    near = jnp.concatenate([near[0:8] + near[8:16] + near[16:24], near[24:32]], axis=0)
    for load in loads[3:]:
        load.wait()
    info_out[0, :, : 3 * atoms] = pos[0]
    for m in range(3):
        info_out[0, :, (3 + m) * atoms : (4 + m) * atoms] = vel[m]
    info_out[0, :, 6 * atoms : 7 * atoms] = kind[...].astype(F32)
    info_out[0, :, 7 * atoms :] = jnp.concatenate(
        [jnp.broadcast_to(owner_ref[:, b : b + 1], (1, 128)) for b in range(atoms // 128)], axis=1
    ).astype(F32)
    info_copies = [
        push(j, info_out.at[0], info_in.at[j], info_send, info_recv, (0, 0, -j)) for j in range(1, zs)
    ]
    for copy in info_copies:
        copy.start()
    prepare(weights, w_scratch)

    for copy in pos_copies:
        copy.wait()
    rows = []
    for m in range(3):
        cut = slice(m * atoms, (m + 1) * atoms)
        for k in range(SLOTS):
            rows.append(pos[0, :, cut] if leader[k] == home else halo[leader[k], :, cut])
        rows.append(jnp.zeros((32 - SLOTS, atoms), F32))
    table = jnp.concatenate(split3(jnp.concatenate(rows, axis=0)), axis=0)

    by_slot, by_centre = gradient(
        table, near, pair, live_ref[...], w_scratch, (mem_t, nbr_t), store
    )

    members = {k: [j for j in range(SLOTS) if leader[j] == k] for k in leaders + [home]}
    pieces = {}
    for step, k in first.items():
        parts = []
        for m in range(3):
            row = by_slot[32 * m + k : 32 * m + k + 1]
            for j in members[k][1:]:
                row = row + by_slot[32 * m + j : 32 * m + j + 1]
            parts.append(row - by_centre[m : m + 1] if k == home else row)
        pieces[step] = parts
    nothing = [jnp.zeros((1, atoms), F32)] * 3

    force_copies = []
    for t, (x, y, z) in enumerate(partners):
        for j in range(zs):
            for m, row in enumerate(pieces.get((x, y, (z + j) % zs), nothing)):
                lane = (3 * j + m) * atoms
                force_out[t, :, lane : lane + atoms] = row
        copy = push(t, force_out.at[t], force_in.at[t], force_send, force_recv, (x, y, z))
        copy.start()
        force_copies.append(copy)
    for copy in info_copies + force_copies:
        copy.wait()
    arrived = force_in[0]
    for t in range(1, len(partners)):
        arrived = arrived + force_in[t]
    is_z = (lax.broadcasted_iota(jnp.int32, (9, 128), 0) == 2).astype(F32)
    myself = me[2].astype(F32)
    for j in range(zs):
        about = info_out[0] if j == 0 else info_in[j]
        part = pieces.get((0, 0, j), nothing)
        forces = -jnp.concatenate(
            [part[m] + arrived[:, (3 * j + m) * atoms : (3 * j + m + 1) * atoms] for m in range(3)], axis=0
        )
        place = jnp.concatenate([about[:, m * atoms : (m + 1) * atoms] for m in range(3)], axis=0)
        speed = jnp.concatenate([about[:, (3 + m) * atoms : (4 + m) * atoms] for m in range(3)], axis=0)
        new_vel = speed + TIME_STEP * forces * (1.0 / (1.0 + about[:, 6 * atoms : 7 * atoms]))
        new_pos = place + TIME_STEP * new_vel
        state = jnp.concatenate([new_pos, new_vel, forces], axis=0)
        source = lax.rem(me[2] + j, zs)
        lift = is_z * ((source - me[2]).astype(F32) * float(atoms // 64))
        result = jnp.zeros((9, 128), F32)
        for b in range(atoms // 128):
            owner = about[:, 7 * atoms + 128 * b : 7 * atoms + 128 * b + 128]
            mine = jnp.broadcast_to(owner, (9, 128)) == myself
            result = result + jnp.where(mine, state[:, 128 * b : 128 * b + 128] + lift, 0.0)
        out[source] = result


def per_device(
    sizes,
    positions,
    velocities,
    species,
    pair_table,
    live_blocks,
    owners,
    radial_weight,
    center_embed,
    neighbour_embed,
    vector_weight,
    env_weight,
    vector_gate,
    latent_weight,
    energy_weight,
):
    atoms = positions.shape[4]
    count = pair_table.shape[4]
    width = latent_weight.shape[1]
    ch = vector_weight.shape[0]
    zs = sizes[2]
    dma = pltpu.SemaphoreType.DMA
    senders = len(owners_of_pieces(sizes))
    operands = (
        pair_table.reshape(3, 1, count),
        species.reshape(1, atoms),
        positions.reshape(1, 1, 3 * atoms),
        live_blocks.reshape(1, 1),
        velocities.reshape(3, 1, atoms),
        owners.reshape(1, -1),
        radial_weight.T,
        center_embed.T,
        neighbour_embed.T,
        vector_weight.T,
        env_weight,
        vector_gate,
        jnp.swapaxes(latent_weight, 1, 2),
        energy_weight.reshape(1, width),
    )
    result = pl.pallas_call(
        functools.partial(kernel, sizes),
        out_shape=jax.ShapeDtypeStruct((zs, 9, 128), F32),
        in_specs=[pl.BlockSpec(memory_space=pl.ANY)] * 14,
        out_specs=pl.BlockSpec(memory_space=pltpu.VMEM),
        scratch_shapes=weight_scratch(width, ch)
        + store_scratch(width, ch, count, atoms)
        + [
            pltpu.VMEM((atoms, count), BF16),
            pltpu.VMEM((atoms, count), BF16),
            pltpu.VMEM((SLOTS, 1, 3 * atoms), F32),
            pltpu.VMEM((senders, 1, 3 * zs * atoms), F32),
            pltpu.VMEM((senders, 1, 3 * zs * atoms), F32),
            pltpu.VMEM((1, 1, 8 * atoms), F32),
            pltpu.VMEM((zs, 1, 8 * atoms), F32),
            dma((SLOTS,)),
            dma((SLOTS,)),
            dma((senders,)),
            dma((senders,)),
            dma((zs,)),
            dma((zs,)),
            dma((14,)),
        ]
        + [pltpu.VMEM(v.shape, v.dtype) for v in operands],
        compiler_params=pltpu.CompilerParams(
            collective_id=0, has_side_effects=True, vmem_limit_bytes=60 << 20
        ),
    )(*operands)
    return result[None, None, None]


def solution(mesh):
    sizes = (mesh.shape["gx"], mesh.shape["gy"], mesh.shape["gz"])
    spread = ("gx", "gy", "gz")
    in_specs = (
        P(*spread, None, None),
        P(*spread, None, None),
        P(*spread, None),
        P(*spread, None, None),
        P(*spread),
        P(*spread, None),
    ) + (P(),) * 8
    return jax.shard_map(
        functools.partial(per_device, sizes),
        mesh=mesh,
        in_specs=in_specs,
        out_specs=P(*spread, None, None, None),
        check_vma=False,
    )
```
